128 devices in a mesh: gx: 8 (over x, core), gy: 4 (over y), gz: 4 (over z).
Axes of the slice: x: 4, y: 4, z: 4, core: 2. Of those that a mesh axis runs over, the one named last changes fastest.
Arguments:
- tokens: bfloat16 [16384, 7168], P(('gx', 'gz'), 'gy'), may hold values from -6 to 6
- grad_out: bfloat16 [16384, 7168], P(('gx', 'gz'), 'gy'), may hold values from -6 to 6
- slot_token: int32 [32, 8, 32], P(('gx', 'gz')), may hold values from 0 to 511, as said below
- slot_count: int32 [32, 8], P(('gx', 'gz')), may hold values from 0 to 32, as said below
- slot_score: bfloat16 [32, 8, 32], P(('gx', 'gz')), may hold values from 0.099609375 to 1
- gate_weight: bfloat16 [8, 7168, 2048], P('gx', 'gy', 'gz'), may hold values from -0.0625 to 0.0625
- up_weight: bfloat16 [8, 7168, 2048], P('gx', 'gy', 'gz'), may hold values from -0.0625 to 0.0625
- down_weight: bfloat16 [8, 2048, 7168], P('gx', 'gz', 'gy'), may hold values from -0.125 to 0.125
Outputs:
- input_grad: bfloat16 [16384, 7168], P(('gx', 'gz'), 'gy')
- score_grad: float32 [32, 8, 32], P(('gx', 'gz'))
- gate_grad: bfloat16 [8, 7168, 2048], P('gx', 'gy', 'gz')
- up_grad: bfloat16 [8, 7168, 2048], P('gx', 'gy', 'gz')
- down_grad: bfloat16 [8, 2048, 7168], P('gx', 'gz', 'gy')
The draws below stay inside these ranges and needn't reach their ends.
Inputs may be any that keep to these rules, and one draw needn't show every extreme that they name: `slot_token`: for each group and expert the 32 indices are distinct. `slot_count`: slots at or beyond the count are not used; their indices and weights play no part.
All inputs are finite; a program needn't handle non-finite values.
Results may differ from the reference program's by a relative error of at most 0.0075.
Values may be sent and summed in bfloat16 or wider, within the bound.
No kernel may reach another device: no remote copies, remote signals or barrier semaphores. Data moves between devices by JAX's collectives and lax.ppermute only.
A program may use at most 128 MiB of HBM per device.

```python
import math
import jax
import jax.numpy as jnp
from jax import lax

D = 7168
FF = 2048
TOK_GRP = 512
MOST = 32
EXPERTS = 8
GROUPS = 32
TOKENS = 16384


def draw_slot_token(key, part):
    key = jax.random.fold_in(key, 11)
    subkeys = jax.random.split(key, GROUPS * EXPERTS)

    def choose_slots(single):
        return jax.random.permutation(single, TOK_GRP)[:MOST]
    chosen = jax.vmap(choose_slots)(subkeys)
    return chosen.reshape(GROUPS, EXPERTS, MOST).astype(jnp.int32)


def draw_slot_count(key, part):
    key = jax.random.fold_in(key, 23)
    hot_key, second = jax.random.split(key)
    hot_expert = jax.random.randint(hot_key, (), 0, EXPERTS)
    background = jax.random.randint(second, (GROUPS, EXPERTS), 0, MOST // 2 + 1)
    column = jnp.arange(EXPERTS)[None, :]
    return jnp.where(column == hot_expert, MOST, background).astype(jnp.int32)


def block_scale(stream_key, extent, cuts, least, top_value):
    def one(position, parts):
        heights = jax.random.uniform(jax.random.fold_in(jax.random.fold_in(stream_key, 6), position), (parts,), jnp.float32, least / len(cuts), top_value / len(cuts))
        return jnp.repeat(jnp.exp(heights), extent[position] // parts).reshape((-1,) + (1,) * (len(extent) - position - 1))

    level = one(*cuts[0])
    for cut in cuts[1:]:
        level = level * one(*cut)
    return level


def noise(stream_key, dims, width, bound, shards=(), kind=jnp.bfloat16):
    array = jax.random.normal(stream_key, dims, jnp.float32) * width
    if len(shards) > 0:
        array = block_scale(stream_key, dims, shards, -0.22, 0.18) * array
    return jnp.clip(array, min=-bound, max=bound).astype(kind)


def setup_inputs(seed: int = 0) -> dict:
    key_of = jax.random.split(jax.random.key(seed), 9)
    return {
        "tokens": noise(key_of[0], (TOKENS, D), 1.0, 6.0, ((0, 32), (1, 4))),
        "grad_out": noise(key_of[1], (TOKENS, D), 1.0, 6.0, ((0, 32), (1, 4))),
        "slot_token": draw_slot_token(jax.random.fold_in(key_of[8], 71), 0),
        "slot_count": draw_slot_count(jax.random.fold_in(key_of[8], 71), 0),
        "slot_score": jnp.clip(jnp.exp(math.log(1.0) - 2.306499 * jax.random.uniform(key_of[4], (GROUPS, EXPERTS, MOST), jnp.float32) ** block_scale(key_of[4], (GROUPS, EXPERTS, MOST), ((0, 32),), -0.2, 0.2)), 0.099609375, 1.0).astype(jnp.bfloat16),
        "gate_weight": noise(key_of[5], (EXPERTS, D, FF), D ** -0.5, 0.0625, ((0, 8), (1, 4), (2, 4))),
        "up_weight": noise(key_of[6], (EXPERTS, D, FF), D ** -0.5, 0.0625, ((0, 8), (1, 4), (2, 4))),
        "down_weight": noise(key_of[7], (EXPERTS, FF, D), FF ** -0.5, 0.125, ((0, 8), (1, 4), (2, 4))),
    }


def expert_pass(x_rows, g_rows, s_rows, w_gate, w_up, w_down):
    gate_value = jnp.dot(x_rows, w_gate, preferred_element_type=jnp.float32)
    up_value = jnp.dot(x_rows, w_up, preferred_element_type=jnp.float32)
    pulled = jnp.dot(g_rows, w_down.T, preferred_element_type=jnp.float32)
    sigmoid_gate = jax.nn.sigmoid(gate_value)
    activated = gate_value * sigmoid_gate
    hidden = (activated * up_value).astype(jnp.bfloat16)
    score_part = jnp.sum(hidden.astype(jnp.float32) * pulled, axis=1)
    hidden_grad = s_rows[:, None] * pulled
    gate_rows = (hidden_grad * up_value * sigmoid_gate * (1.0 + gate_value * (1.0 - sigmoid_gate))).astype(jnp.bfloat16)
    up_rows = (hidden_grad * activated).astype(jnp.bfloat16)
    scaled = (s_rows[:, None] * g_rows.astype(jnp.float32)).astype(jnp.bfloat16)
    down_grad = jnp.dot(hidden.T, scaled, preferred_element_type=jnp.float32)
    gate_grad = jnp.dot(x_rows.T, gate_rows, preferred_element_type=jnp.float32)
    up_grad = jnp.dot(x_rows.T, up_rows, preferred_element_type=jnp.float32)
    row_grad = jnp.dot(gate_rows, w_gate.T, preferred_element_type=jnp.float32) + jnp.dot(up_rows, w_up.T, preferred_element_type=jnp.float32)
    return row_grad, score_part, gate_grad, up_grad, down_grad


def reference(tokens, grad_out, slot_token, slot_count, slot_score, gate_weight, up_weight, down_weight):
    usable = jnp.arange(MOST, dtype=jnp.int32)[None, None, :] < slot_count[:, :, None]
    offsets = (jnp.arange(GROUPS, dtype=jnp.int32) * TOK_GRP)[:, None, None]
    indices = (slot_token + offsets).astype(jnp.int32)
    by_expert = jnp.transpose(indices, (1, 0, 2)).reshape(EXPERTS, GROUPS * MOST)
    usable_expert = jnp.transpose(usable, (1, 0, 2)).reshape(EXPERTS, GROUPS * MOST)
    scores_expert = jnp.transpose(slot_score, (1, 0, 2)).reshape(EXPERTS, GROUPS * MOST)
    zero_value = jnp.zeros((), tokens.dtype)

    def per_expert(expert):
        rows_here = by_expert[expert]
        mask_here = usable_expert[expert]
        x_rows = jnp.where(mask_here[:, None], tokens[rows_here], zero_value)
        g_rows = jnp.where(mask_here[:, None], grad_out[rows_here], zero_value)
        s_rows = jnp.where(mask_here, scores_expert[expert], jnp.zeros((), slot_score.dtype)).astype(jnp.float32)
        return expert_pass(x_rows, g_rows, s_rows, gate_weight[expert], up_weight[expert], down_weight[expert])

    row_grad, score_part, gate_grad, up_grad, down_grad = lax.map(per_expert, jnp.arange(EXPERTS, dtype=jnp.int32))
    total = jnp.zeros((TOKENS, D), jnp.float32).at[by_expert.reshape(-1)].add(row_grad.reshape(-1, D))
    input_grad = total.astype(jnp.bfloat16)
    score_grad = jnp.transpose(score_part.reshape(EXPERTS, GROUPS, MOST), (1, 0, 2))
    return (input_grad, score_grad, gate_grad.astype(jnp.bfloat16), up_grad.astype(jnp.bfloat16), down_grad.astype(jnp.bfloat16))
```

```python
import jax
import jax.numpy as jnp
from jax import lax
from jax.sharding import PartitionSpec as P

CONTRACT_LAST = (((1,), (1,)), ((), ()))
CONTRACT_FIRST = (((0,), (0,)), ((), ()))


def dot(left, right, dims=(((1,), (0,)), ((), ()))):
    return lax.dot_general(left, right, dims, preferred_element_type=jnp.float32)


def shift(array, steps):
    size = lax.axis_size("gz")
    return lax.ppermute(array, "gz", [(i, (i + steps) % size) for i in range(size)])


def ring_gather(own):
    half = own.shape[0] // 2
    before = shift(own, 1)
    after = shift(own, -1)
    far_top = shift(before[:half], 1)
    far_bottom = shift(after[half:], -1)
    return jnp.concatenate([own, before, after, far_top, far_bottom])


def activate(gate_value, up_value, hidden_grad):
    sigmoid_gate = jax.nn.sigmoid(gate_value)
    activated = gate_value * sigmoid_gate
    hidden = (activated * up_value).astype(jnp.bfloat16)
    score_part = jnp.sum(hidden.astype(jnp.float32) * hidden_grad, axis=1)
    gate_rows = (
        hidden_grad * up_value * sigmoid_gate * (1.0 + gate_value * (1.0 - sigmoid_gate))
    ).astype(jnp.bfloat16)
    up_rows = (hidden_grad * activated).astype(jnp.bfloat16)
    return hidden, score_part, gate_rows, up_rows


def local(
    tokens, grad_out, slot_token, slot_count, slot_score, gate_weight, up_weight, down_weight
):
    bf16 = jnp.bfloat16
    chosen = slot_token[0]
    counts = slot_count[0]
    experts, slots = chosen.shape
    group, width = tokens.shape
    usable = jnp.arange(slots, dtype=jnp.int32)[None, :] < counts[:, None]
    score = slot_score[0]
    picked = (
        chosen[:, :, None] == jnp.arange(group, dtype=jnp.int32)[None, None, :]
    ) & usable[:, :, None]
    zero = jnp.zeros((), bf16)
    pick = jnp.where(picked, jnp.ones((), bf16), zero).reshape(experts * slots, group)
    pick_scaled = jnp.where(picked, score[:, :, None], zero).reshape(experts * slots, group)

    w_cat = jnp.concatenate([gate_weight[0], up_weight[0]], axis=1)
    w_down = down_weight[0]
    hidden_units = w_down.shape[0]

    def to_expert(rows):
        return lax.all_to_all(rows, "gx", split_axis=0, concat_axis=0, tiled=True)

    x_own = to_expert(dot(pick, tokens).astype(bf16))
    g_own = to_expert(dot(pick_scaled, grad_out).astype(bf16))
    x_rows = ring_gather(x_own)
    gate_up = lax.psum(dot(x_rows, w_cat).astype(bf16), "gy")
    g_rows = ring_gather(g_own)
    pulled_part = dot(g_rows, w_down, CONTRACT_LAST).astype(bf16)
    gate_up, pulled_part = lax.optimization_barrier((gate_up, pulled_part))
    gate_up = gate_up.astype(jnp.float32)
    pulled = lax.psum(pulled_part, "gy").astype(jnp.float32)
    hidden, score_part, gate_rows, up_rows = activate(
        gate_up[:, :hidden_units], gate_up[:, hidden_units:], pulled
    )
    both_rows = jnp.concatenate([gate_rows, up_rows], axis=1)
    row_part = dot(both_rows, w_cat, CONTRACT_LAST)
    own_rows = x_own.shape[0]

    def piece(k):
        return row_part[k * own_rows : (k + 1) * own_rows]

    f32 = jnp.float32
    total = piece(0)
    total = total + shift(piece(3).astype(bf16), 2).astype(f32)
    total = total + shift(piece(1).astype(bf16), -1).astype(f32)
    total = total + shift(piece(2).astype(bf16), 1).astype(f32)
    back_rows = to_expert(total.astype(bf16))
    input_grad = dot(pick, back_rows, CONTRACT_FIRST).astype(bf16)

    gate_grad = dot(x_rows, gate_rows, CONTRACT_FIRST).astype(bf16)
    up_grad = dot(x_rows, up_rows, CONTRACT_FIRST).astype(bf16)
    down_grad = dot(hidden, g_rows, CONTRACT_FIRST).astype(bf16)

    gz = lax.axis_index("gz")
    gz_count = lax.axis_size("gz")
    relative = score_part.reshape(gz_count, -1)
    place = lax.rem(gz - jnp.arange(gz_count) + gz_count, gz_count)
    order = jnp.array([0, 1, 3, 2], jnp.int32)
    match = place[:, None] == order[None, :]
    absolute = jnp.sum(jnp.where(match[:, :, None], relative[None], 0.0), axis=1)
    absolute = absolute.reshape(gz_count, -1, slots).transpose(1, 0, 2).reshape(-1, slots)
    back_score = lax.all_to_all(absolute, ("gx", "gz"), split_axis=0, concat_axis=0, tiled=True)
    back_score = jnp.sum(back_score.reshape(experts, gz_count, slots), axis=1)
    score_grad = jnp.where(usable, back_score / score.astype(f32), 0.0)[None]
    return input_grad, score_grad, gate_grad[None], up_grad[None], down_grad[None]


def solution(mesh):
    in_specs = (
        P(("gx", "gz"), "gy"),
        P(("gx", "gz"), "gy"),
        P(("gx", "gz"), None, None),
        P(("gx", "gz"), None),
        P(("gx", "gz"), None, None),
        P("gx", "gy", "gz"),
        P("gx", "gy", "gz"),
        P("gx", "gz", "gy"),
    )
    out_specs = (
        P(("gx", "gz"), "gy"),
        P(("gx", "gz"), None, None),
        P("gx", "gy", "gz"),
        P("gx", "gy", "gz"),
        P("gx", "gz", "gy"),
    )
    return jax.shard_map(local, mesh=mesh, in_specs=in_specs, out_specs=out_specs, check_vma=False)
```

```python
import jax
import jax.numpy as jnp
from jax import lax
from jax.sharding import PartitionSpec as P

CONTRACT_LAST = (((1,), (1,)), ((), ()))
CONTRACT_FIRST = (((0,), (0,)), ((), ()))
CHUNKS = 2
BF16 = jnp.bfloat16
F32 = jnp.float32


def dot(left, right, dims=(((1,), (0,)), ((), ()))):
    return lax.dot_general(left, right, dims, preferred_element_type=F32)


def shift(array, steps):
    size = lax.axis_size("gz")
    return lax.ppermute(array, "gz", [(i, (i + steps) % size) for i in range(size)])


def swap(array, bit):
    if bit:
        pairs = [(1, 2), (2, 1), (3, 0), (0, 3)]
    else:
        pairs = [(0, 1), (1, 0), (2, 3), (3, 2)]
    return lax.ppermute(array, "gy", pairs)


def add(left, right):
    return left.astype(F32) + right.astype(F32)


def fence(*arrays):
    return lax.optimization_barrier(arrays)


def to_experts(rows):
    return lax.all_to_all(rows, "gx", split_axis=0, concat_axis=0, tiled=True)


def activate(values, units):
    gate_value, up_value, hidden_grad = (
        values[:, :units],
        values[:, units : 2 * units],
        values[:, 2 * units :],
    )
    sigmoid_gate = jax.nn.sigmoid(gate_value)
    activated = gate_value * sigmoid_gate
    hidden = (activated * up_value).astype(BF16)
    score_part = jnp.sum(hidden.astype(F32) * hidden_grad, axis=1)
    gate_rows = (
        hidden_grad * up_value * sigmoid_gate * (1.0 + gate_value * (1.0 - sigmoid_gate))
    ).astype(BF16)
    up_rows = (hidden_grad * activated).astype(BF16)
    return hidden, score_part, jnp.concatenate([gate_rows, up_rows], axis=1)


def local(
    tokens, grad_out, slot_token, slot_count, slot_score, gate_weight, up_weight, down_weight
):
    chosen = slot_token[0]
    counts = slot_count[0]
    experts, slots = chosen.shape
    group, width = tokens.shape
    usable = jnp.arange(slots, dtype=jnp.int32)[None, :] < counts[:, None]
    score = slot_score[0]
    picked = (
        chosen[:, :, None] == jnp.arange(group, dtype=jnp.int32)[None, None, :]
    ) & usable[:, :, None]
    zero = jnp.zeros((), BF16)
    pick = jnp.where(picked, jnp.ones((), BF16), zero)
    pick_scaled = jnp.where(picked, score[:, :, None], zero)

    w_down = down_weight[0]
    units = w_down.shape[0]
    part_slots = slots // CHUNKS
    own_rows = experts * part_slots
    half = own_rows // 2

    def chunk_of(array, c):
        return array[:, c * part_slots : (c + 1) * part_slots].reshape(own_rows, -1)

    def partial(rows):
        return jnp.concatenate(
            [
                dot(rows[:, :width], w_cat).astype(BF16),
                dot(rows[:, width:], w_down, CONTRACT_LAST).astype(BF16),
            ],
            axis=1,
        )

    picks = [chunk_of(pick, c) for c in range(CHUNKS)]
    scaled_picks = [chunk_of(pick_scaled, c) for c in range(CHUNKS)]

    def dispatch(pick_x, pick_g):
        return jnp.concatenate(
            [dot(pick_x, tokens).astype(BF16), dot(pick_g, grad_out).astype(BF16)], axis=1
        )

    def row_parts(act):
        part = dot(act[2], w_cat, CONTRACT_LAST).astype(BF16)
        return part[:own_rows], part[own_rows:]

    sent0 = dispatch(picks[0], scaled_picks[0])
    own0 = to_experts(sent0)
    sent0, pick1 = fence(sent0, picks[1])
    sent1 = dispatch(pick1, scaled_picks[1])
    sent1, gate_weight, up_weight = fence(sent1, gate_weight, up_weight)
    w_cat = jnp.concatenate([gate_weight[0], up_weight[0]], axis=1)
    own0, sent1, w_cat = fence(own0, sent1, w_cat)
    before0, after0 = shift(own0, 1), shift(own0, -1)
    own1 = to_experts(sent1)
    part0 = partial(own0)
    own1, part0 = fence(own1, part0)
    before1, after1 = shift(own1, 1), shift(own1, -1)
    part1 = partial(own1)
    own_top, own_bottom = swap(part0, 0), swap(part1, 1)
    before0, after0, part0, part1 = fence(before0, after0, part0, part1)
    far_top0, far_bottom0 = shift(before0[:half], 1), shift(after0[half:], -1)
    own_top, own_bottom, before0, after0 = fence(own_top, own_bottom, before0, after0)
    part0, part1 = add(part0, own_top).astype(BF16), add(part1, own_bottom).astype(BF16)
    own_top, own_bottom = swap(part0, 1), swap(part1, 0)
    before1, after1, part0, part1 = fence(before1, after1, part0, part1)
    far_top1, far_bottom1 = shift(before1[:half], 1), shift(after1[half:], -1)
    far_top0, far_bottom0, before1, after1 = fence(far_top0, far_bottom0, before1, after1)
    top0 = jnp.concatenate([before0, far_top0])
    bottom0 = jnp.concatenate([after0, far_bottom0])
    top_part0, bottom_part0 = partial(top0), partial(bottom0)
    top_in0, bottom_in0 = swap(top_part0, 0), swap(bottom_part0, 1)
    own_top, own_bottom, top_part0, bottom_part0 = fence(
        own_top, own_bottom, top_part0, bottom_part0
    )
    own_acts = [activate(add(part0, own_top), units), activate(add(part1, own_bottom), units)]
    own_part0 = dot(own_acts[0][2], w_cat, CONTRACT_LAST).astype(BF16)
    own_part1 = dot(own_acts[1][2], w_cat, CONTRACT_LAST).astype(BF16)
    top_in0, bottom_in0, own_part0, own_part1 = fence(top_in0, bottom_in0, own_part0, own_part1)
    top_part0 = add(top_part0, top_in0).astype(BF16)
    bottom_part0 = add(bottom_part0, bottom_in0).astype(BF16)
    top_in0, bottom_in0 = swap(top_part0, 1), swap(bottom_part0, 0)
    far_top1, far_bottom1, top_part0, bottom_part0 = fence(
        far_top1, far_bottom1, top_part0, bottom_part0
    )
    top1 = jnp.concatenate([before1, far_top1])
    bottom1 = jnp.concatenate([after1, far_bottom1])
    top_part1, bottom_part1 = partial(top1), partial(bottom1)
    top_in1, bottom_in1 = swap(top_part1, 0), swap(bottom_part1, 1)
    top_in0, bottom_in0, top_part1, bottom_part1 = fence(
        top_in0, bottom_in0, top_part1, bottom_part1
    )
    top_act0 = activate(add(top_part0, top_in0), units)
    bottom_act0 = activate(add(bottom_part0, bottom_in0), units)
    near_top0, far_top0 = row_parts(top_act0)
    near_bottom0, far_bottom0 = row_parts(bottom_act0)
    from_top0, from_bottom0 = shift(far_top0, -1), shift(far_bottom0, 1)
    top_in1, bottom_in1, near_top0, near_bottom0 = fence(
        top_in1, bottom_in1, near_top0, near_bottom0
    )
    top_part1 = add(top_part1, top_in1).astype(BF16)
    bottom_part1 = add(bottom_part1, bottom_in1).astype(BF16)
    top_in1, bottom_in1 = swap(top_part1, 1), swap(bottom_part1, 0)
    from_top0, from_bottom0, top_part1, bottom_part1 = fence(
        from_top0, from_bottom0, top_part1, bottom_part1
    )

    def joined(near_top, near_bottom, from_top, from_bottom):
        before_sum = jnp.concatenate(
            [add(near_top[:half], from_top).astype(BF16), near_top[half:]]
        )
        after_sum = jnp.concatenate(
            [near_bottom[:half], add(near_bottom[half:], from_bottom).astype(BF16)]
        )
        return before_sum, after_sum

    before_sum0, after_sum0 = joined(near_top0, near_bottom0, from_top0, from_bottom0)
    home_top0, home_bottom0 = shift(before_sum0, -1), shift(after_sum0, 1)
    top_in1, bottom_in1, before_sum0, after_sum0 = fence(
        top_in1, bottom_in1, before_sum0, after_sum0
    )
    top_act1 = activate(add(top_part1, top_in1), units)
    bottom_act1 = activate(add(bottom_part1, bottom_in1), units)
    near_top1, far_top1 = row_parts(top_act1)
    near_bottom1, far_bottom1 = row_parts(bottom_act1)
    from_top1, from_bottom1 = shift(far_top1, -1), shift(far_bottom1, 1)
    home_top0, home_bottom0, near_top1, near_bottom1 = fence(
        home_top0, home_bottom0, near_top1, near_bottom1
    )
    total0 = own_part0.astype(F32) + add(home_top0, home_bottom0)
    total0 = total0.astype(BF16)
    back0 = to_experts(total0)
    from_top1, from_bottom1, total0 = fence(from_top1, from_bottom1, total0)
    before_sum1, after_sum1 = joined(near_top1, near_bottom1, from_top1, from_bottom1)
    home_top1, home_bottom1 = shift(before_sum1, -1), shift(after_sum1, 1)

    own, tops, bottoms = [own0, own1], [top0, top1], [bottom0, bottom1]
    top_acts, bottom_acts = [top_act0, top_act1], [bottom_act0, bottom_act1]
    groups = own + tops + bottoms
    acts = own_acts + top_acts + bottom_acts
    all_rows = jnp.concatenate(groups)
    hidden = jnp.concatenate([a[0] for a in acts])
    both_rows = jnp.concatenate([a[2] for a in acts])
    before_sum1, after_sum1, all_rows, hidden, both_rows = fence(
        before_sum1, after_sum1, all_rows, hidden, both_rows
    )
    gate_grad = dot(all_rows[:, :width], both_rows[:, :units], CONTRACT_FIRST).astype(BF16)
    up_grad = dot(all_rows[:, :width], both_rows[:, units:], CONTRACT_FIRST).astype(BF16)
    home_top1, home_bottom1, gate_grad, up_grad, back0 = fence(
        home_top1, home_bottom1, gate_grad, up_grad, back0
    )
    total1 = own_part1.astype(F32) + add(home_top1, home_bottom1)
    total1 = total1.astype(BF16)
    back1 = to_experts(total1)
    total1, hidden = fence(total1, hidden)
    down_grad = dot(hidden, all_rows[:, width:], CONTRACT_FIRST).astype(BF16)
    back1, down_grad = fence(back1, down_grad)
    input_grad = dot(
        jnp.concatenate(picks), jnp.concatenate([back0, back1]), CONTRACT_FIRST
    ).astype(BF16)

    gz = lax.axis_index("gz")
    gz_count = lax.axis_size("gz")
    relative = []
    for c in range(CHUNKS):
        o, t, b = own_acts[c][1], top_acts[c][1], bottom_acts[c][1]
        relative.append(
            jnp.stack(
                [o, t[:own_rows], jnp.concatenate([t[own_rows:], b[own_rows:]]), b[:own_rows]]
            ).reshape(gz_count, experts, part_slots)
        )
    relative = jnp.concatenate(relative, axis=2)
    place = lax.rem(gz - jnp.arange(gz_count) + gz_count, gz_count)
    match = place[:, None] == jnp.arange(gz_count)[None, :]
    absolute = jnp.sum(jnp.where(match[:, :, None, None], relative[None], 0.0), axis=1)
    absolute = absolute.transpose(1, 0, 2).reshape(-1, slots)
    back_score = lax.all_to_all(absolute, ("gx", "gz"), split_axis=0, concat_axis=0, tiled=True)
    back_score = jnp.sum(back_score.reshape(experts, gz_count, slots), axis=1)
    score_grad = jnp.where(usable, back_score / score.astype(F32), 0.0)[None]
    return input_grad, score_grad, gate_grad[None], up_grad[None], down_grad[None]


def solution(mesh):
    in_specs = (
        P(("gx", "gz"), "gy"),
        P(("gx", "gz"), "gy"),
        P(("gx", "gz"), None, None),
        P(("gx", "gz"), None),
        P(("gx", "gz"), None, None),
        P("gx", "gy", "gz"),
        P("gx", "gy", "gz"),
        P("gx", "gz", "gy"),
    )
    out_specs = (
        P(("gx", "gz"), "gy"),
        P(("gx", "gz"), None, None),
        P("gx", "gy", "gz"),
        P("gx", "gy", "gz"),
        P("gx", "gz", "gy"),
    )
    return jax.shard_map(local, mesh=mesh, in_specs=in_specs, out_specs=out_specs, check_vma=False)
```

```python
import functools
import jax
import jax.numpy as jnp
from jax import lax
from jax.experimental import pallas as pl
from jax.experimental.pallas import tpu as pltpu
from jax.sharding import PartitionSpec as P

CONTRACT_LAST = (((1,), (1,)), ((), ()))
CONTRACT_FIRST = (((0,), (0,)), ((), ()))
CHUNKS = 2
LANES = 128
VMEM_LIMIT = 20 * 1024 * 1024
BF16 = jnp.bfloat16
F32 = jnp.float32


def dot(left, right, dims=(((1,), (0,)), ((), ()))):
    return lax.dot_general(left, right, dims, preferred_element_type=F32)


def shift(array, steps):
    size = lax.axis_size("gz")
    return lax.ppermute(array, "gz", [(i, (i + steps) % size) for i in range(size)])


def swap(array, bit):
    if bit:
        pairs = [(1, 2), (2, 1), (3, 0), (0, 3)]
    else:
        pairs = [(0, 1), (1, 0), (2, 3), (3, 2)]
    return lax.ppermute(array, "gy", pairs)


def add(left, right):
    return left.astype(F32) + right.astype(F32)


def fence(*arrays):
    return lax.optimization_barrier(arrays)


def to_experts(rows):
    return lax.all_to_all(rows, "gx", split_axis=0, concat_axis=0, tiled=True)


def call(kernel, outs, scratch, args, flops, aliases=None, free=(), in_hbm=(), out_hbm=()):
    vmem, hbm = pl.BlockSpec(memory_space=pltpu.VMEM), pl.BlockSpec(memory_space=pltpu.HBM)
    return pl.pallas_call(
        kernel,
        out_shape=[
            pltpu.HBM(*o) if i in out_hbm else jax.ShapeDtypeStruct(*o)
            for i, o in enumerate(outs)
        ],
        in_specs=[
            hbm if i in in_hbm else pl.BlockSpec(memory_space=pl.ANY) if i in free else vmem
            for i in range(len(args))
        ],
        out_specs=[hbm if i in out_hbm else vmem for i in range(len(outs))],
        scratch_shapes=scratch,
        input_output_aliases=aliases or {},
        cost_estimate=pl.CostEstimate(flops=1, bytes_accessed=1, transcendentals=0),
        compiler_params=pltpu.CompilerParams(vmem_limit_bytes=VMEM_LIMIT),
    )(*args)


def partial_kernel(pieces, base, aliased, *refs):
    inputs, refs = refs[:pieces], refs[pieces:]
    weights = refs[:3]
    refs = refs[4:] if aliased else refs[3:]
    *outs, all_rows, rows, w_gate, w_up, w_down, sems, w_sems = refs
    width, units = w_gate.shape
    at, copies = 0, []
    for i, piece in enumerate(inputs):
        place = pl.ds(at, piece.shape[0])
        copies.append(pltpu.make_async_copy(piece, rows.at[place], sems.at[i]))
        at += piece.shape[0]
    held = (w_gate, w_up, w_down)
    w_copies = [pltpu.make_async_copy(weights[i], held[i], w_sems.at[i]) for i in range(3)]
    for copy in copies + w_copies:
        copy.start()
    for copy in copies:
        copy.wait()
    keep = pltpu.make_async_copy(rows, all_rows.at[pl.ds(base, at)], sems.at[pieces])
    keep.start()
    size = at // len(outs)

    def store(k, part):
        for i, out in enumerate(outs):
            out[:, k * units : (k + 1) * units] = part[i * size : (i + 1) * size].astype(BF16)

    w_copies[0].wait()
    store(0, dot(rows[:, :width], w_gate[...]))
    w_copies[1].wait()
    store(1, dot(rows[:, :width], w_up[...]))
    w_copies[2].wait()
    store(2, dot(rows[:, width:], w_down[...], CONTRACT_LAST))
    keep.wait()


def partial(pieces, weights, all_rows, base, total_rows, parts):
    count = sum(p.shape[0] for p in pieces)
    width, units = weights[0].shape
    n = len(pieces)
    args = list(pieces) + list(weights)
    aliases, in_hbm = {}, (n, n + 1, n + 2)
    if all_rows is not None:
        aliases, in_hbm = {len(args): parts}, (n, n + 1, n + 2, n + 3)
        args.append(all_rows)
    return call(
        functools.partial(partial_kernel, n, base, all_rows is not None),
        [((count // parts, 3 * units), BF16)] * parts + [((total_rows, 2 * width), BF16)],
        [pltpu.VMEM((count, 2 * width), BF16)]
        + [pltpu.VMEM(w.shape, BF16) for w in weights]
        + [pltpu.SemaphoreType.DMA((n + 1,)), pltpu.SemaphoreType.DMA((3,))],
        args,
        6 * count * width * units,
        aliases,
        tuple(range(n)),
        in_hbm,
        (parts,),
    )


def add_kernel(top, top_in, bottom, bottom_in, top_out, bottom_out):
    top_out[...] = add(top[...], top_in[...]).astype(BF16)
    bottom_out[...] = add(bottom[...], bottom_in[...]).astype(BF16)


def add_halves(top, top_in, bottom, bottom_in):
    return call(
        add_kernel,
        [(top.shape, BF16), (bottom.shape, BF16)],
        [],
        [top, top_in, bottom, bottom_in],
        2 * top.size,
    )


def two_parts(score):
    high = score.astype(BF16).astype(F32)
    lane = lax.broadcasted_iota(jnp.int32, (score.shape[0], LANES), 1)
    return jnp.where(lane == 0, high, jnp.where(lane == 1, score - high, 0.0)).astype(BF16)


def act_kernel(base, near, aliased, *refs):
    top, top_in, bottom, bottom_in = refs[:4]
    weights = refs[4:6]
    refs = refs[8:] if aliased else refs[6:]
    *outs, all_hidden, all_both, hidden_rows, both_rows, w_gate, w_up, sems = refs
    width, units = w_gate.shape
    half = top.shape[0]
    w_copies = [
        pltpu.make_async_copy(weights[0], w_gate, sems.at[2]),
        pltpu.make_async_copy(weights[1], w_up, sems.at[3]),
    ]
    for copy in w_copies:
        copy.start()
    score_parts = []
    for start, own, arrived in ((0, top, top_in), (half, bottom, bottom_in)):
        gate_value = add(own[:, :units], arrived[:, :units])
        up_value = add(own[:, units : 2 * units], arrived[:, units : 2 * units])
        hidden_grad = add(own[:, 2 * units :], arrived[:, 2 * units :])
        sigmoid_gate = jax.nn.sigmoid(gate_value)
        activated = gate_value * sigmoid_gate
        hidden = (activated * up_value).astype(BF16)
        score_part = jnp.sum(hidden.astype(F32) * hidden_grad, axis=1, keepdims=True)
        score_parts.append(two_parts(score_part))
        hidden_rows[start : start + half] = hidden
        both_rows[start : start + half, :units] = (
            hidden_grad * up_value * sigmoid_gate * (1.0 + gate_value * (1.0 - sigmoid_gate))
        ).astype(BF16)
        both_rows[start : start + half, units:] = (hidden_grad * activated).astype(BF16)
    place = pl.ds(base, 2 * half)
    copies = [
        pltpu.make_async_copy(hidden_rows, all_hidden.at[place], sems.at[0]),
        pltpu.make_async_copy(both_rows, all_both.at[place], sems.at[1]),
    ]
    for copy in copies:
        copy.start()
    for copy in w_copies:
        copy.wait()
    part = dot(both_rows[:, :units], w_gate[...], CONTRACT_LAST)
    part = (part + dot(both_rows[:, units:], w_up[...], CONTRACT_LAST)).astype(BF16)
    outs[0][:, :width] = part[:near]
    outs[1][:, :width] = part[half : half + near]
    outs[0][:, width:] = score_parts[0][:near]
    outs[1][:, width:] = score_parts[1][:near]
    if near < half:
        far = half - near
        outs[2][:far, :width] = part[near:half]
        outs[2][far:, :width] = part[half + near :]
        outs[2][:far, width:] = score_parts[0][near:]
        outs[2][far:, width:] = score_parts[1][near:]
    for copy in copies:
        copy.wait()


def act(top, top_in, bottom, bottom_in, weights, gathered, base, near, total_rows):
    width, units = weights[0].shape
    half = top.shape[0]
    args = [top, top_in, bottom, bottom_in, weights[0], weights[1]]
    outs = [((near, width + LANES), BF16)] * 2
    if near < half:
        outs.append(((2 * (half - near), width + LANES), BF16))
    n = len(outs)
    outs += [((total_rows, units), BF16), ((total_rows, 2 * units), BF16)]
    aliases, in_hbm = {}, (4, 5)
    if gathered is not None:
        aliases, in_hbm = {6: n, 7: n + 1}, (4, 5, 6, 7)
        args += list(gathered)
    return call(
        functools.partial(act_kernel, base, near, gathered is not None),
        outs,
        [
            pltpu.VMEM((2 * half, units), BF16),
            pltpu.VMEM((2 * half, 2 * units), BF16),
            pltpu.VMEM((width, units), BF16),
            pltpu.VMEM((width, units), BF16),
            pltpu.SemaphoreType.DMA((4,)),
        ],
        args,
        8 * half * width * units,
        aliases,
        (),
        in_hbm,
        (n, n + 1),
    )


def total_kernel(width, own, first, second, third, out):
    total = add(own[...], first[...]) + add(second[...], third[...])
    out[:, :width] = total[:, :width].astype(BF16)
    out[:, width:] = two_parts(jnp.sum(total[:, width:], axis=1, keepdims=True))


def total_of(own, first, second, third):
    kernel = functools.partial(total_kernel, own.shape[1] - LANES)
    return call(kernel, [(own.shape, BF16)], [], [own, first, second, third], 4 * own.size)[0]


def local(
    tokens, grad_out, slot_token, slot_count, slot_score, gate_weight, up_weight, down_weight
):
    chosen = slot_token[0]
    counts = slot_count[0]
    experts, slots = chosen.shape
    group, width = tokens.shape
    usable = jnp.arange(slots, dtype=jnp.int32)[None, :] < counts[:, None]
    score = slot_score[0]
    picked = (
        chosen[:, :, None] == jnp.arange(group, dtype=jnp.int32)[None, None, :]
    ) & usable[:, :, None]
    zero = jnp.zeros((), BF16)
    pick = jnp.where(picked, jnp.ones((), BF16), zero)
    pick_scaled = jnp.where(picked, score[:, :, None], zero)

    weights = [
        pltpu.with_memory_space_constraint(w[0], pltpu.HBM)
        for w in (gate_weight, up_weight, down_weight)
    ]
    units = weights[2].shape[0]
    part_slots = slots // CHUNKS
    own_rows = experts * part_slots
    half = own_rows // 2
    total_rows = own_rows * CHUNKS * lax.axis_size("gz")

    def chunk_of(array, c):
        return array[:, c * part_slots : (c + 1) * part_slots].reshape(own_rows, -1)

    picks = [chunk_of(pick, c) for c in range(CHUNKS)]
    scaled_picks = [chunk_of(pick_scaled, c) for c in range(CHUNKS)]

    def dispatch(pick_x, pick_g):
        return jnp.concatenate(
            [dot(pick_x, tokens).astype(BF16), dot(pick_g, grad_out).astype(BF16)], axis=1
        )

    sent0 = dispatch(picks[0], scaled_picks[0])
    own0 = to_experts(sent0)
    sent0, pick1 = fence(sent0, picks[1])
    sent1 = dispatch(pick1, scaled_picks[1])
    own0, sent1 = fence(own0, sent1)
    before0, after0 = shift(own0, 1), shift(own0, -1)
    own1 = to_experts(sent1)
    own_top, all_rows = partial((own0,), weights, None, 0, total_rows, 1)
    own_top_in = swap(own_top, 0)
    before0, after0, own1, all_rows = fence(before0, after0, own1, all_rows)
    cut_top0, cut_bottom0 = before0[:half], after0[half:]
    far_top0, far_bottom0 = shift(cut_top0, 1), shift(cut_bottom0, -1)
    own1, all_rows, cut_top0, cut_bottom0 = fence(own1, all_rows, cut_top0, cut_bottom0)
    own_bottom, all_rows = partial((own1,), weights, all_rows, own_rows, total_rows, 1)
    own_bottom_in = swap(own_bottom, 1)
    far_top0, far_bottom0, all_rows, own1 = fence(far_top0, far_bottom0, all_rows, own1)
    before1, after1 = shift(own1, 1), shift(own1, -1)
    own_top_in, own_bottom_in, far_top0 = fence(own_top_in, own_bottom_in, far_top0)
    own_top, own_bottom = add_halves(own_top, own_top_in, own_bottom, own_bottom_in)
    own_top_in, own_bottom_in = swap(own_top, 1), swap(own_bottom, 0)
    own_top, all_rows = fence(own_top, all_rows)
    base0, base1 = CHUNKS * own_rows, (CHUNKS + 3) * own_rows
    top0, bottom0, all_rows = partial(
        (before0, far_top0, after0, far_bottom0), weights, all_rows, base0, total_rows, 2
    )
    own_top_in, own_bottom_in, top0, bottom0 = fence(own_top_in, own_bottom_in, top0, bottom0)
    top_in0, bottom_in0 = swap(top0, 0), swap(bottom0, 1)
    own_part0, own_part1, *gathered = act(
        own_top, own_top_in, own_bottom, own_bottom_in, weights, None, 0, own_rows, total_rows
    )
    before1, after1, own_part0 = fence(before1, after1, own_part0)
    cut_top1, cut_bottom1 = before1[:half], after1[half:]
    far_top1, far_bottom1 = shift(cut_top1, 1), shift(cut_bottom1, -1)
    top_in0, bottom_in0, cut_top1, cut_bottom1 = fence(
        top_in0, bottom_in0, cut_top1, cut_bottom1
    )
    top0, bottom0 = add_halves(top0, top_in0, bottom0, bottom_in0)
    top_in0, bottom_in0 = swap(top0, 1), swap(bottom0, 0)
    far_top1, far_bottom1, top0, bottom0 = fence(far_top1, far_bottom1, top0, bottom0)
    top1, bottom1, all_rows = partial(
        (before1, far_top1, after1, far_bottom1), weights, all_rows, base1, total_rows, 2
    )
    top_in1, bottom_in1 = swap(top1, 0), swap(bottom1, 1)
    top_in0, bottom_in0, all_rows = fence(top_in0, bottom_in0, all_rows)
    near_top0, near_bottom0, far0, *gathered = act(
        top0, top_in0, bottom0, bottom_in0, weights, gathered, base0, own_rows, total_rows
    )
    home0 = [shift(near_top0, -1), shift(near_bottom0, 1), shift(far0, 2)]
    top_in1, bottom_in1, far0 = fence(top_in1, bottom_in1, far0)
    top1, bottom1 = add_halves(top1, top_in1, bottom1, bottom_in1)
    top_in1, bottom_in1 = swap(top1, 1), swap(bottom1, 0)
    top_in1, bottom_in1, top1, bottom1, *home0 = fence(
        top_in1, bottom_in1, top1, bottom1, *home0
    )
    near_top1, near_bottom1, far1, *gathered = act(
        top1, top_in1, bottom1, bottom_in1, weights, gathered, base1, own_rows, total_rows
    )
    home1 = [shift(near_top1, -1), shift(near_bottom1, 1), shift(far1, 2)]
    *home0, far1 = fence(*home0, far1)
    total0 = total_of(own_part0, *home0)
    back0 = to_experts(total0)
    all_hidden, all_both = gathered
    total0, all_rows, all_hidden, all_both = fence(total0, all_rows, all_hidden, all_both)
    gate_grad = dot(all_rows[:, :width], all_both[:, :units], CONTRACT_FIRST).astype(BF16)
    up_grad = dot(all_rows[:, :width], all_both[:, units:], CONTRACT_FIRST).astype(BF16)
    *home1, gate_grad, up_grad, back0 = fence(*home1, gate_grad, up_grad, back0)
    total1 = total_of(own_part1, *home1)
    back1 = to_experts(total1)
    total1, all_hidden = fence(total1, all_hidden)
    down_grad = dot(all_hidden, all_rows[:, width:], CONTRACT_FIRST).astype(BF16)
    back1, down_grad = fence(back1, down_grad)
    back = jnp.concatenate([back0, back1])
    input_grad = dot(jnp.concatenate(picks), back[:, :width], CONTRACT_FIRST).astype(BF16)
    back_score = jnp.sum(back[:, width : width + 2].astype(F32), axis=1)
    back_score = back_score.reshape(CHUNKS, experts, part_slots).transpose(1, 0, 2)
    back_score = back_score.reshape(experts, slots)
    score_grad = jnp.where(usable, back_score / score.astype(F32), 0.0)[None]
    return input_grad, score_grad, gate_grad[None], up_grad[None], down_grad[None]


def solution(mesh):
    in_specs = (
        P(("gx", "gz"), "gy"),
        P(("gx", "gz"), "gy"),
        P(("gx", "gz"), None, None),
        P(("gx", "gz"), None),
        P(("gx", "gz"), None, None),
        P("gx", "gy", "gz"),
        P("gx", "gy", "gz"),
        P("gx", "gz", "gy"),
    )
    out_specs = (
        P(("gx", "gz"), "gy"),
        P(("gx", "gz"), None, None),
        P("gx", "gy", "gz"),
        P("gx", "gy", "gz"),
        P("gx", "gz", "gy"),
    )
    return jax.shard_map(local, mesh=mesh, in_specs=in_specs, out_specs=out_specs, check_vma=False)
```

```python
import functools
import jax
import jax.numpy as jnp
from jax import lax
from jax.experimental import pallas as pl
from jax.experimental.pallas import tpu as pltpu
from jax.sharding import PartitionSpec as P

CONTRACT_MIDDLE = (((1,), (0,)), ((), ()))
CONTRACT_LAST = (((1,), (1,)), ((), ()))
CONTRACT_FIRST = (((0,), (0,)), ((), ()))
CHUNKS = 2
LANES = 128
TOTAL_FLOPS = 20_000_000_000
VMEM_LIMIT = 20 * 1024 * 1024
BF16 = jnp.bfloat16
F32 = jnp.float32


def dot(left, right, dims=CONTRACT_MIDDLE):
    return lax.dot_general(left, right, dims, preferred_element_type=F32)


def shift(array, steps):
    size = lax.axis_size("gz")
    return lax.ppermute(array, "gz", [(i, (i + steps) % size) for i in range(size)])


def swap(array, bit):
    if bit:
        pairs = [(1, 2), (2, 1), (3, 0), (0, 3)]
    else:
        pairs = [(0, 1), (1, 0), (2, 3), (3, 2)]
    return lax.ppermute(array, "gy", pairs)


def add(left, right):
    return left.astype(F32) + right.astype(F32)


def fence(*arrays):
    return lax.optimization_barrier(arrays)


def to_experts(rows):
    return lax.all_to_all(rows, "gx", split_axis=0, concat_axis=0, tiled=True)


def call(kernel, outs, scratch, args, aliases=None, free=(), in_hbm=(), out_hbm=(), flops=1):
    vmem, hbm = pl.BlockSpec(memory_space=pltpu.VMEM), pl.BlockSpec(memory_space=pltpu.HBM)
    return pl.pallas_call(
        kernel,
        out_shape=[
            pltpu.HBM(*o) if i in out_hbm else jax.ShapeDtypeStruct(*o)
            for i, o in enumerate(outs)
        ],
        in_specs=[
            hbm if i in in_hbm else pl.BlockSpec(memory_space=pl.ANY) if i in free else vmem
            for i in range(len(args))
        ],
        out_specs=[hbm if i in out_hbm else vmem for i in range(len(outs))],
        scratch_shapes=scratch,
        input_output_aliases=aliases or {},
        cost_estimate=pl.CostEstimate(flops=flops, bytes_accessed=1, transcendentals=0),
        compiler_params=pltpu.CompilerParams(vmem_limit_bytes=VMEM_LIMIT),
    )(*args)


def hold_kernel(*refs):
    count = len(refs) // 2
    copies = [
        pltpu.make_async_copy(refs[i], refs[count + i], refs[-1].at[i]) for i in range(count)
    ]
    for copy in copies:
        copy.start()
    for copy in copies:
        copy.wait()


def hold(arrays):
    copies = pl.pallas_call(
        hold_kernel,
        out_shape=[pltpu.VMEM(a.shape, a.dtype) for a in arrays],
        in_specs=[pl.BlockSpec(memory_space=pltpu.HBM)] * len(arrays),
        out_specs=[pl.BlockSpec(memory_space=pltpu.VMEM)] * len(arrays),
        scratch_shapes=[pltpu.SemaphoreType.DMA((len(arrays),))],
        compiler_params=pltpu.CompilerParams(vmem_limit_bytes=VMEM_LIMIT),
    )(*arrays)
    return [pltpu.with_memory_space_constraint(a, pltpu.VMEM) for a in copies]


def partial_kernel(pieces, base, aliased, held, *refs):
    inputs, refs = refs[:pieces], refs[pieces:]
    weights = refs[:3]
    refs = refs[4:] if aliased else refs[3:]
    if held:
        *outs, all_rows, rows, sems = refs
    else:
        *outs, all_rows, rows, sems, w_gate, w_up, w_down, w_sems = refs
        copies = [
            pltpu.make_async_copy(w, v, w_sems.at[i])
            for i, (w, v) in enumerate(zip(weights, (w_gate, w_up, w_down)))
        ]
        weights = (w_gate, w_up, w_down)
    w_copies = [] if held else copies
    width, units = weights[0].shape
    at, copies = 0, []
    for i, piece in enumerate(inputs):
        place = pl.ds(at, piece.shape[0])
        copies.append(pltpu.make_async_copy(piece, rows.at[place], sems.at[i]))
        at += piece.shape[0]
    for copy in copies + w_copies:
        copy.start()
    for copy in copies:
        copy.wait()
    keep = pltpu.make_async_copy(rows, all_rows.at[pl.ds(base, at)], sems.at[pieces])
    keep.start()
    size = at // len(outs)

    def store(k, left, dims):
        if not held:
            w_copies[k].wait()
        part = dot(left, weights[k][...], dims)
        for i, out in enumerate(outs):
            out[:, k * units : (k + 1) * units] = part[i * size : (i + 1) * size].astype(BF16)

    store(0, rows[:, :width], CONTRACT_MIDDLE)
    store(1, rows[:, :width], CONTRACT_MIDDLE)
    store(2, rows[:, width:], CONTRACT_LAST)
    keep.wait()


def partial(pieces, weights, all_rows, base, total_rows, held):
    count = sum(p.shape[0] for p in pieces)
    width, units = weights[0].shape
    n = len(pieces)
    args = list(pieces) + list(weights)
    aliases, in_hbm = {}, () if held else (n, n + 1, n + 2)
    if all_rows is not None:
        aliases, in_hbm = {len(args): 2}, in_hbm + (n + 3,)
        args.append(all_rows)
    scratch = [pltpu.VMEM((count, 2 * width), BF16), pltpu.SemaphoreType.DMA((n + 1,))]
    if not held:
        scratch += [pltpu.VMEM(w.shape, BF16) for w in weights]
        scratch.append(pltpu.SemaphoreType.DMA((3,)))
    return call(
        functools.partial(partial_kernel, n, base, all_rows is not None, held),
        [((count // 2, 3 * units), BF16)] * 2 + [((total_rows, 2 * width), BF16)],
        scratch,
        args,
        aliases,
        tuple(range(n)),
        in_hbm,
        (2,),
    )


def add_kernel(top, top_in, bottom, bottom_in, top_out, bottom_out):
    top_out[...] = add(top[...], top_in[...]).astype(BF16)
    bottom_out[...] = add(bottom[...], bottom_in[...]).astype(BF16)


def add_halves(top, top_in, bottom, bottom_in):
    return call(
        add_kernel,
        [(top.shape, BF16), (bottom.shape, BF16)],
        [],
        [top, top_in, bottom, bottom_in],
    )


def two_parts(score):
    high = score.astype(BF16).astype(F32)
    lane = lax.broadcasted_iota(jnp.int32, (score.shape[0], LANES), 1)
    return jnp.where(lane == 0, high, jnp.where(lane == 1, score - high, 0.0)).astype(BF16)


def act_kernel(pairs, base, layout, aliased, *refs):
    values, refs = refs[: 2 * pairs], refs[2 * pairs :]
    w_gate, w_up = refs[:2]
    refs = refs[4:] if aliased else refs[2:]
    *outs, all_hidden, all_both, hidden_rows, both_rows, sems = refs
    width, units = w_gate.shape
    size = values[0].shape[0]
    scores = []
    for i in range(pairs):
        own, arrived = values[2 * i], values[2 * i + 1]
        place = slice(i * size, (i + 1) * size)
        gate_value = add(own[:, :units], arrived[:, :units])
        up_value = add(own[:, units : 2 * units], arrived[:, units : 2 * units])
        hidden_grad = add(own[:, 2 * units :], arrived[:, 2 * units :])
        sigmoid_gate = jax.nn.sigmoid(gate_value)
        activated = gate_value * sigmoid_gate
        hidden = (activated * up_value).astype(BF16)
        score_part = jnp.sum(hidden.astype(F32) * hidden_grad, axis=1, keepdims=True)
        scores.append(two_parts(score_part))
        hidden_rows[place] = hidden
        both_rows[place, :units] = (
            hidden_grad * up_value * sigmoid_gate * (1.0 + gate_value * (1.0 - sigmoid_gate))
        ).astype(BF16)
        both_rows[place, units:] = (hidden_grad * activated).astype(BF16)
    place = pl.ds(base, pairs * size)
    copies = [
        pltpu.make_async_copy(hidden_rows, all_hidden.at[place], sems.at[0]),
        pltpu.make_async_copy(both_rows, all_both.at[place], sems.at[1]),
    ]
    for copy in copies:
        copy.start()
    part = dot(both_rows[:, :units], w_gate[...], CONTRACT_LAST)
    part = (part + dot(both_rows[:, units:], w_up[...], CONTRACT_LAST)).astype(BF16)
    for out, blocks in zip(outs, layout):
        at = 0
        for i, first, last in blocks:
            end = at + last - first
            out[at:end, :width] = part[i * size + first : i * size + last]
            out[at:end, width:] = scores[i][first:last]
            at = end
    for copy in copies:
        copy.wait()


def act(pairs, weights, gathered, base, layout, total_rows):
    width, units = weights[0].shape
    rows = sum(own.shape[0] for own, _ in pairs)
    args = [a for pair in pairs for a in pair] + [weights[0], weights[1]]
    outs = [
        ((sum(last - first for _, first, last in blocks), width + LANES), BF16)
        for blocks in layout
    ]
    n = len(outs)
    outs += [((total_rows, units), BF16), ((total_rows, 2 * units), BF16)]
    aliases, in_hbm = {}, ()
    if gathered is not None:
        in_hbm = (len(args), len(args) + 1)
        aliases = {in_hbm[0]: n, in_hbm[1]: n + 1}
        args += list(gathered)
    return call(
        functools.partial(act_kernel, len(pairs), base, layout, gathered is not None),
        outs,
        [
            pltpu.VMEM((rows, units), BF16),
            pltpu.VMEM((rows, 2 * units), BF16),
            pltpu.SemaphoreType.DMA((2,)),
        ],
        args,
        aliases,
        (),
        in_hbm,
        (n, n + 1),
    )


def total_kernel(width, own, first, second, third, out):
    total = add(own[...], first[...]) + add(second[...], third[...])
    out[:, :width] = total[:, :width].astype(BF16)
    out[:, width:] = two_parts(jnp.sum(total[:, width:], axis=1, keepdims=True))


def total_of(own, first, second, third, flops=1):
    kernel = functools.partial(total_kernel, own.shape[1] - LANES)
    args = [own, first, second, third]
    return call(kernel, [(own.shape, BF16)], [], args, flops=flops)[0]


def final_kernel(chunks, usable, score, *refs):
    picks, backs = refs[:chunks], refs[chunks : 2 * chunks]
    input_grad, score_grad = refs[2 * chunks :]
    width = input_grad.shape[1]
    experts, slots = score.shape
    rows = backs[0].shape[0]
    part_slots = rows // experts
    total = sum(dot(p[...], b[:, :width], CONTRACT_FIRST) for p, b in zip(picks, backs))
    input_grad[...] = total.astype(BF16)
    row = lax.broadcasted_iota(jnp.int32, (rows, slots), 0)
    column = lax.broadcasted_iota(jnp.int32, (rows, slots), 1)
    expert = (
        lax.broadcasted_iota(jnp.int32, (experts, rows), 1) // part_slots
        == lax.broadcasted_iota(jnp.int32, (experts, rows), 0)
    ).astype(F32).astype(BF16)
    table = jnp.zeros((experts, slots), F32)
    for c, back in enumerate(backs):
        for k in range(2):
            value = back[:, width + k : width + k + 1].astype(F32)
            spread = jnp.where(column == c * part_slots + row % part_slots, value, 0.0)
            table += dot(expert, spread.astype(BF16))
    score_grad[...] = jnp.where(usable[...] > 0, table / score[...], 0.0)


def final(usable, score, picks, backs):
    group, width = picks[0].shape[1], backs[0].shape[1] - LANES
    return call(
        functools.partial(final_kernel, len(picks)),
        [((group, width), BF16), (score.shape, F32)],
        [],
        [usable.astype(jnp.int32), score.astype(F32), *picks, *backs],
    )


def local(
    tokens, grad_out, slot_token, slot_count, slot_score, gate_weight, up_weight, down_weight
):
    chosen = slot_token[0]
    counts = slot_count[0]
    experts, slots = chosen.shape
    group, width = tokens.shape
    usable = jnp.arange(slots, dtype=jnp.int32)[None, :] < counts[:, None]
    score = slot_score[0]
    picked = (
        chosen[:, :, None] == jnp.arange(group, dtype=jnp.int32)[None, None, :]
    ) & usable[:, :, None]
    zero = jnp.zeros((), BF16)
    pick = jnp.where(picked, jnp.ones((), BF16), zero)
    pick_scaled = jnp.where(picked, score[:, :, None], zero)

    weights = [
        pltpu.with_memory_space_constraint(w[0], pltpu.HBM)
        for w in (gate_weight, up_weight, down_weight)
    ]
    units = weights[2].shape[0]
    part_slots = slots // CHUNKS
    own_rows = experts * part_slots
    half = own_rows // 2
    total_rows = own_rows * CHUNKS * lax.axis_size("gz")

    def chunk_of(array, c):
        return array[:, c * part_slots : (c + 1) * part_slots].reshape(own_rows, -1)

    picks = [chunk_of(pick, c) for c in range(CHUNKS)]
    scaled_picks = [chunk_of(pick_scaled, c) for c in range(CHUNKS)]

    def dispatch(pick_x, pick_g):
        return jnp.concatenate(
            [dot(pick_x, tokens).astype(BF16), dot(pick_g, grad_out).astype(BF16)], axis=1
        )

    sent0 = dispatch(picks[0], scaled_picks[0])
    own0 = to_experts(sent0)
    sent0, pick1 = fence(sent0, picks[1])
    sent1 = dispatch(pick1, scaled_picks[1])
    own0, sent1 = fence(own0, sent1)
    before0, after0 = shift(own0, 1), shift(own0, -1)
    own1 = to_experts(sent1)
    a_top, a_bottom, all_rows = partial((own0,), weights, None, 0, total_rows, False)
    a_top_in, a_bottom_in = swap(a_top, 0), swap(a_bottom, 1)
    a_top, a_bottom = add_halves(a_top, a_top_in, a_bottom, a_bottom_in)
    a_top_in, a_bottom_in = swap(a_top, 1), swap(a_bottom, 0)
    own1, all_rows, a_top = fence(own1, all_rows, a_top)
    b_top, b_bottom, all_rows = partial((own1,), weights, all_rows, own_rows, total_rows, False)
    a_top_in, a_bottom_in, b_top, b_bottom = fence(a_top_in, a_bottom_in, b_top, b_bottom)
    b_top_in, b_bottom_in = swap(b_top, 0), swap(b_bottom, 1)
    before0, after0, b_top = fence(before0, after0, b_top)
    cut_top0, cut_bottom0 = before0[:half], after0[half:]
    far_top0, far_bottom0 = shift(cut_top0, 1), shift(cut_bottom0, -1)
    cut_top0, cut_bottom0, *weights = fence(cut_top0, cut_bottom0, *weights)
    held = hold(weights)
    b_top_in, b_bottom_in, cut_top0, cut_bottom0, *held = fence(
        b_top_in, b_bottom_in, cut_top0, cut_bottom0, *held
    )
    b_top, b_bottom = add_halves(b_top, b_top_in, b_bottom, b_bottom_in)
    b_top_in, b_bottom_in = swap(b_top, 1), swap(b_bottom, 0)
    far_top0, far_bottom0, b_top, b_bottom, own1 = fence(
        far_top0, far_bottom0, b_top, b_bottom, own1
    )
    before1, after1 = shift(own1, 1), shift(own1, -1)
    base0, base1 = CHUNKS * own_rows, (CHUNKS + 3) * own_rows
    top0, bottom0, all_rows = partial(
        (before0, far_top0, after0, far_bottom0), held, all_rows, base0, total_rows, True
    )
    b_top_in, b_bottom_in, top0, bottom0 = fence(b_top_in, b_bottom_in, top0, bottom0)
    top_in0, bottom_in0 = swap(top0, 0), swap(bottom0, 1)
    own_pairs = [
        (a_top, a_top_in),
        (a_bottom, a_bottom_in),
        (b_top, b_top_in),
        (b_bottom, b_bottom_in),
    ]
    own_layout = (((0, 0, half), (1, 0, half)), ((2, 0, half), (3, 0, half)))
    own_part0, own_part1, *gathered = act(own_pairs, held, None, 0, own_layout, total_rows)
    before1, after1, own_part0 = fence(before1, after1, own_part0)
    cut_top1, cut_bottom1 = before1[:half], after1[half:]
    far_top1, far_bottom1 = shift(cut_top1, 1), shift(cut_bottom1, -1)
    top_in0, bottom_in0, cut_top1, cut_bottom1 = fence(
        top_in0, bottom_in0, cut_top1, cut_bottom1
    )
    top0, bottom0 = add_halves(top0, top_in0, bottom0, bottom_in0)
    top_in0, bottom_in0 = swap(top0, 1), swap(bottom0, 0)
    far_top1, far_bottom1, top0, bottom0 = fence(far_top1, far_bottom1, top0, bottom0)
    top1, bottom1, all_rows = partial(
        (before1, far_top1, after1, far_bottom1), held, all_rows, base1, total_rows, True
    )
    top_in1, bottom_in1 = swap(top1, 0), swap(bottom1, 1)
    top_in0, bottom_in0, all_rows = fence(top_in0, bottom_in0, all_rows)
    layout = (
        ((0, 0, own_rows),),
        ((1, 0, own_rows),),
        ((0, own_rows, own_rows + half), (1, own_rows, own_rows + half)),
    )
    near_top0, near_bottom0, far0, *gathered = act(
        [(top0, top_in0), (bottom0, bottom_in0)], held, gathered, base0, layout, total_rows
    )
    home0 = [shift(near_top0, -1), shift(near_bottom0, 1), shift(far0, 2)]
    top_in1, bottom_in1, far0 = fence(top_in1, bottom_in1, far0)
    top1, bottom1 = add_halves(top1, top_in1, bottom1, bottom_in1)
    top_in1, bottom_in1 = swap(top1, 1), swap(bottom1, 0)
    *home0, top1, bottom1 = fence(*home0, top1, bottom1)
    total0 = total_of(own_part0, *home0, flops=TOTAL_FLOPS)
    top_in1, bottom_in1, top1, total0 = fence(top_in1, bottom_in1, top1, total0)
    near_top1, near_bottom1, far1, *gathered = act(
        [(top1, top_in1), (bottom1, bottom_in1)], held, gathered, base1, layout, total_rows
    )
    total0, far1 = fence(total0, far1)
    home1 = [shift(near_top1, -1), shift(near_bottom1, 1), shift(far1, 2)]
    back0 = to_experts(total0)
    all_hidden, all_both = gathered
    total0, all_rows, all_hidden, all_both = fence(total0, all_rows, all_hidden, all_both)
    gate_grad = dot(all_rows[:, :width], all_both[:, :units], CONTRACT_FIRST).astype(BF16)
    up_grad = dot(all_rows[:, :width], all_both[:, units:], CONTRACT_FIRST).astype(BF16)
    *home1, gate_grad, up_grad = fence(*home1, gate_grad, up_grad)
    total1 = total_of(own_part1, *home1)
    total1, back0 = fence(total1, back0)
    back1 = to_experts(total1)
    total1, all_hidden = fence(total1, all_hidden)
    down_grad = dot(all_hidden, all_rows[:, width:], CONTRACT_FIRST).astype(BF16)
    back1, down_grad = fence(back1, down_grad)
    input_grad, score_grad = final(usable, score, picks, [back0, back1])
    return input_grad, score_grad[None], gate_grad[None], up_grad[None], down_grad[None]


def solution(mesh):
    in_specs = (
        P(("gx", "gz"), "gy"),
        P(("gx", "gz"), "gy"),
        P(("gx", "gz"), None, None),
        P(("gx", "gz"), None),
        P(("gx", "gz"), None, None),
        P("gx", "gy", "gz"),
        P("gx", "gy", "gz"),
        P("gx", "gz", "gy"),
    )
    out_specs = (
        P(("gx", "gz"), "gy"),
        P(("gx", "gz"), None, None),
        P("gx", "gy", "gz"),
        P("gx", "gy", "gz"),
        P("gx", "gz", "gy"),
    )
    return jax.shard_map(local, mesh=mesh, in_specs=in_specs, out_specs=out_specs, check_vma=False)
```

```python
import functools
import jax
import jax.numpy as jnp
from jax import lax
from jax.experimental import pallas as pl
from jax.experimental.pallas import tpu as pltpu
from jax.sharding import PartitionSpec as P

CONTRACT_MIDDLE = (((1,), (0,)), ((), ()))
CONTRACT_LAST = (((1,), (1,)), ((), ()))
CONTRACT_FIRST = (((0,), (0,)), ((), ()))
CHUNKS = 2
LANES = 128
PARTIAL_FLOPS = 20000000000
TOTAL_FLOPS = 20_000_000_000
VMEM_LIMIT = 20 * 1024 * 1024
BF16 = jnp.bfloat16
F32 = jnp.float32


def dot(left, right, dims=CONTRACT_MIDDLE):
    return lax.dot_general(left, right, dims, preferred_element_type=F32)


def shift(array, steps):
    size = lax.axis_size("gz")
    return lax.ppermute(array, "gz", [(i, (i + steps) % size) for i in range(size)])


def swap(array, bit):
    if bit:
        pairs = [(1, 2), (2, 1), (3, 0), (0, 3)]
    else:
        pairs = [(0, 1), (1, 0), (2, 3), (3, 2)]
    return lax.ppermute(array, "gy", pairs)


def add(left, right):
    return left.astype(F32) + right.astype(F32)


def fence(*arrays):
    return lax.optimization_barrier(arrays)


def to_experts(rows):
    return lax.all_to_all(rows, "gx", split_axis=0, concat_axis=0, tiled=True)


def call(kernel, outs, scratch, args, aliases=None, free=(), in_hbm=(), out_hbm=(), flops=1):
    vmem, hbm = pl.BlockSpec(memory_space=pltpu.VMEM), pl.BlockSpec(memory_space=pltpu.HBM)
    return pl.pallas_call(
        kernel,
        out_shape=[
            pltpu.HBM(*o) if i in out_hbm else jax.ShapeDtypeStruct(*o)
            for i, o in enumerate(outs)
        ],
        in_specs=[
            hbm if i in in_hbm else pl.BlockSpec(memory_space=pl.ANY) if i in free else vmem
            for i in range(len(args))
        ],
        out_specs=[hbm if i in out_hbm else vmem for i in range(len(outs))],
        scratch_shapes=scratch,
        input_output_aliases=aliases or {},
        cost_estimate=pl.CostEstimate(flops=flops, bytes_accessed=1, transcendentals=0),
        compiler_params=pltpu.CompilerParams(vmem_limit_bytes=VMEM_LIMIT),
    )(*args)


def hold_kernel(*refs):
    count = len(refs) // 2
    copies = [
        pltpu.make_async_copy(refs[i], refs[count + i], refs[-1].at[i]) for i in range(count)
    ]
    for copy in copies:
        copy.start()
    for copy in copies:
        copy.wait()


def hold(arrays):
    copies = pl.pallas_call(
        hold_kernel,
        out_shape=[pltpu.VMEM(a.shape, a.dtype) for a in arrays],
        in_specs=[pl.BlockSpec(memory_space=pltpu.HBM)] * len(arrays),
        out_specs=[pl.BlockSpec(memory_space=pltpu.VMEM)] * len(arrays),
        scratch_shapes=[pltpu.SemaphoreType.DMA((len(arrays),))],
        compiler_params=pltpu.CompilerParams(vmem_limit_bytes=VMEM_LIMIT),
    )(*arrays)
    return [pltpu.with_memory_space_constraint(a, pltpu.VMEM) for a in copies]


def partial_kernel(pieces, base, aliased, held, *refs):
    inputs, refs = refs[:pieces], refs[pieces:]
    weights = refs[:3]
    refs = refs[4:] if aliased else refs[3:]
    if held:
        *outs, all_rows, rows, sems = refs
    else:
        *outs, all_rows, rows, sems, w_gate, w_up, w_down, w_sems = refs
        copies = [
            pltpu.make_async_copy(w, v, w_sems.at[i])
            for i, (w, v) in enumerate(zip(weights, (w_gate, w_up, w_down)))
        ]
        weights = (w_gate, w_up, w_down)
    w_copies = [] if held else copies
    width, units = weights[0].shape
    at, copies = 0, []
    for i, piece in enumerate(inputs):
        place = pl.ds(at, piece.shape[0])
        copies.append(pltpu.make_async_copy(piece, rows.at[place], sems.at[i]))
        at += piece.shape[0]
    for copy in copies + w_copies:
        copy.start()
    for copy in copies:
        copy.wait()
    keep = pltpu.make_async_copy(rows, all_rows.at[pl.ds(base, at)], sems.at[pieces])
    keep.start()
    size = at // len(outs)

    def store(k, left, dims):
        if not held:
            w_copies[k].wait()
        part = dot(left, weights[k][...], dims)
        for i, out in enumerate(outs):
            out[:, k * units : (k + 1) * units] = part[i * size : (i + 1) * size].astype(BF16)

    store(0, rows[:, :width], CONTRACT_MIDDLE)
    store(1, rows[:, :width], CONTRACT_MIDDLE)
    store(2, rows[:, width:], CONTRACT_LAST)
    keep.wait()


def partial(pieces, weights, all_rows, base, total_rows, held, flops=1):
    count = sum(p.shape[0] for p in pieces)
    width, units = weights[0].shape
    n = len(pieces)
    args = list(pieces) + list(weights)
    aliases, in_hbm = {}, () if held else (n, n + 1, n + 2)
    if all_rows is not None:
        aliases, in_hbm = {len(args): 2}, in_hbm + (n + 3,)
        args.append(all_rows)
    scratch = [pltpu.VMEM((count, 2 * width), BF16), pltpu.SemaphoreType.DMA((n + 1,))]
    if not held:
        scratch += [pltpu.VMEM(w.shape, BF16) for w in weights]
        scratch.append(pltpu.SemaphoreType.DMA((3,)))
    return call(
        functools.partial(partial_kernel, n, base, all_rows is not None, held),
        [((count // 2, 3 * units), BF16)] * 2 + [((total_rows, 2 * width), BF16)],
        scratch,
        args,
        aliases,
        tuple(range(n)),
        in_hbm,
        (2,),
        flops,
    )


def add_kernel(top, top_in, bottom, bottom_in, top_out, bottom_out):
    top_out[...] = add(top[...], top_in[...]).astype(BF16)
    bottom_out[...] = add(bottom[...], bottom_in[...]).astype(BF16)


def add_halves(top, top_in, bottom, bottom_in):
    return call(
        add_kernel,
        [(top.shape, BF16), (bottom.shape, BF16)],
        [],
        [top, top_in, bottom, bottom_in],
    )


def two_parts(score):
    high = score.astype(BF16).astype(F32)
    lane = lax.broadcasted_iota(jnp.int32, (score.shape[0], LANES), 1)
    return jnp.where(lane == 0, high, jnp.where(lane == 1, score - high, 0.0)).astype(BF16)


def act_kernel(pairs, base, layout, aliased, *refs):
    values, refs = refs[: 2 * pairs], refs[2 * pairs :]
    w_gate, w_up = refs[:2]
    refs = refs[4:] if aliased else refs[2:]
    *outs, all_hidden, all_both, hidden_rows, both_rows, sems = refs
    width, units = w_gate.shape
    size = values[0].shape[0]
    scores = []
    for i in range(pairs):
        own, arrived = values[2 * i], values[2 * i + 1]
        place = slice(i * size, (i + 1) * size)
        gate_value = add(own[:, :units], arrived[:, :units])
        up_value = add(own[:, units : 2 * units], arrived[:, units : 2 * units])
        hidden_grad = add(own[:, 2 * units :], arrived[:, 2 * units :])
        sigmoid_gate = jax.nn.sigmoid(gate_value)
        activated = gate_value * sigmoid_gate
        hidden = (activated * up_value).astype(BF16)
        score_part = jnp.sum(hidden.astype(F32) * hidden_grad, axis=1, keepdims=True)
        scores.append(two_parts(score_part))
        hidden_rows[place] = hidden
        both_rows[place, :units] = (
            hidden_grad * up_value * sigmoid_gate * (1.0 + gate_value * (1.0 - sigmoid_gate))
        ).astype(BF16)
        both_rows[place, units:] = (hidden_grad * activated).astype(BF16)
    place = pl.ds(base, pairs * size)
    copies = [
        pltpu.make_async_copy(hidden_rows, all_hidden.at[place], sems.at[0]),
        pltpu.make_async_copy(both_rows, all_both.at[place], sems.at[1]),
    ]
    for copy in copies:
        copy.start()
    part = dot(both_rows[:, :units], w_gate[...], CONTRACT_LAST)
    part = (part + dot(both_rows[:, units:], w_up[...], CONTRACT_LAST)).astype(BF16)
    for out, blocks in zip(outs, layout):
        at = 0
        for i, first, last in blocks:
            end = at + last - first
            out[at:end, :width] = part[i * size + first : i * size + last]
            out[at:end, width:] = scores[i][first:last]
            at = end
    for copy in copies:
        copy.wait()


def act(pairs, weights, gathered, base, layout, total_rows):
    width, units = weights[0].shape
    rows = sum(own.shape[0] for own, _ in pairs)
    args = [a for pair in pairs for a in pair] + [weights[0], weights[1]]
    outs = [
        ((sum(last - first for _, first, last in blocks), width + LANES), BF16)
        for blocks in layout
    ]
    n = len(outs)
    outs += [((total_rows, units), BF16), ((total_rows, 2 * units), BF16)]
    aliases, in_hbm = {}, ()
    if gathered is not None:
        in_hbm = (len(args), len(args) + 1)
        aliases = {in_hbm[0]: n, in_hbm[1]: n + 1}
        args += list(gathered)
    return call(
        functools.partial(act_kernel, len(pairs), base, layout, gathered is not None),
        outs,
        [
            pltpu.VMEM((rows, units), BF16),
            pltpu.VMEM((rows, 2 * units), BF16),
            pltpu.SemaphoreType.DMA((2,)),
        ],
        args,
        aliases,
        (),
        in_hbm,
        (n, n + 1),
    )


def total_kernel(width, own, first, second, third, out):
    total = add(own[...], first[...]) + add(second[...], third[...])
    out[:, :width] = total[:, :width].astype(BF16)
    out[:, width:] = two_parts(jnp.sum(total[:, width:], axis=1, keepdims=True))


def total_of(own, first, second, third, flops=1):
    kernel = functools.partial(total_kernel, own.shape[1] - LANES)
    args = [own, first, second, third]
    return call(kernel, [(own.shape, BF16)], [], args, flops=flops)[0]


def final_kernel(chunks, usable, score, *refs):
    picks, backs = refs[:chunks], refs[chunks : 2 * chunks]
    input_grad, score_grad = refs[2 * chunks :]
    width = input_grad.shape[1]
    experts, slots = score.shape
    rows = backs[0].shape[0]
    part_slots = rows // experts
    total = sum(dot(p[...], b[:, :width], CONTRACT_FIRST) for p, b in zip(picks, backs))
    input_grad[...] = total.astype(BF16)
    row = lax.broadcasted_iota(jnp.int32, (rows, slots), 0)
    column = lax.broadcasted_iota(jnp.int32, (rows, slots), 1)
    expert = (
        lax.broadcasted_iota(jnp.int32, (experts, rows), 1) // part_slots
        == lax.broadcasted_iota(jnp.int32, (experts, rows), 0)
    ).astype(F32).astype(BF16)
    table = jnp.zeros((experts, slots), F32)
    for c, back in enumerate(backs):
        for k in range(2):
            value = back[:, width + k : width + k + 1].astype(F32)
            spread = jnp.where(column == c * part_slots + row % part_slots, value, 0.0)
            table += dot(expert, spread.astype(BF16))
    score_grad[...] = jnp.where(usable[...] > 0, table / score[...], 0.0)


def final(usable, score, picks, backs):
    group, width = picks[0].shape[1], backs[0].shape[1] - LANES
    return call(
        functools.partial(final_kernel, len(picks)),
        [((group, width), BF16), (score.shape, F32)],
        [],
        [usable.astype(jnp.int32), score.astype(F32), *picks, *backs],
    )


def local(
    tokens, grad_out, slot_token, slot_count, slot_score, gate_weight, up_weight, down_weight
):
    chosen = slot_token[0]
    counts = slot_count[0]
    experts, slots = chosen.shape
    group, width = tokens.shape
    usable = jnp.arange(slots, dtype=jnp.int32)[None, :] < counts[:, None]
    score = slot_score[0]
    picked = (
        chosen[:, :, None] == jnp.arange(group, dtype=jnp.int32)[None, None, :]
    ) & usable[:, :, None]
    zero = jnp.zeros((), BF16)
    pick = jnp.where(picked, jnp.ones((), BF16), zero)
    pick_scaled = jnp.where(picked, score[:, :, None], zero)

    weights = [
        pltpu.with_memory_space_constraint(w[0], pltpu.HBM)
        for w in (gate_weight, up_weight, down_weight)
    ]
    units = weights[2].shape[0]
    part_slots = slots // CHUNKS
    own_rows = experts * part_slots
    half = own_rows // 2
    total_rows = own_rows * CHUNKS * lax.axis_size("gz")

    def chunk_of(array, c):
        return array[:, c * part_slots : (c + 1) * part_slots].reshape(own_rows, -1)

    picks = [chunk_of(pick, c) for c in range(CHUNKS)]
    scaled_picks = [chunk_of(pick_scaled, c) for c in range(CHUNKS)]

    def dispatch(pick_x, pick_g):
        return jnp.concatenate(
            [dot(pick_x, tokens).astype(BF16), dot(pick_g, grad_out).astype(BF16)], axis=1
        )

    sent0 = dispatch(picks[0], scaled_picks[0])
    own0 = to_experts(sent0)
    sent0, pick1 = fence(sent0, picks[1])
    sent1 = dispatch(pick1, scaled_picks[1])
    own0, sent1 = fence(own0, sent1)
    before0, after0 = shift(own0, 1), shift(own0, -1)
    own1 = to_experts(sent1)
    a_top, a_bottom, all_rows = partial((own0,), weights, None, 0, total_rows, False)
    a_top_in, a_bottom_in = swap(a_top, 0), swap(a_bottom, 1)
    a_top, a_bottom = add_halves(a_top, a_top_in, a_bottom, a_bottom_in)
    a_top_in, a_bottom_in = swap(a_top, 1), swap(a_bottom, 0)
    own1, all_rows, a_top = fence(own1, all_rows, a_top)
    b_top, b_bottom, all_rows = partial((own1,), weights, all_rows, own_rows, total_rows, False)
    a_top_in, a_bottom_in, b_top, b_bottom = fence(a_top_in, a_bottom_in, b_top, b_bottom)
    b_top_in, b_bottom_in = swap(b_top, 0), swap(b_bottom, 1)
    before0, after0, b_top = fence(before0, after0, b_top)
    cut_top0, cut_bottom0 = before0[:half], after0[half:]
    far_top0, far_bottom0 = shift(cut_top0, 1), shift(cut_bottom0, -1)
    cut_top0, cut_bottom0, *weights = fence(cut_top0, cut_bottom0, *weights)
    held = hold(weights)
    b_top_in, b_bottom_in, cut_top0, cut_bottom0, *held = fence(
        b_top_in, b_bottom_in, cut_top0, cut_bottom0, *held
    )
    b_top, b_bottom = add_halves(b_top, b_top_in, b_bottom, b_bottom_in)
    b_top_in, b_bottom_in = swap(b_top, 1), swap(b_bottom, 0)
    far_top0, far_bottom0, b_top, b_bottom, own1 = fence(
        far_top0, far_bottom0, b_top, b_bottom, own1
    )
    before1, after1 = shift(own1, 1), shift(own1, -1)
    base0, base1 = CHUNKS * own_rows, (CHUNKS + 3) * own_rows
    top0, bottom0, all_rows = partial(
        (before0, far_top0, after0, far_bottom0), held, all_rows, base0, total_rows, True
    )
    b_top_in, b_bottom_in, top0, bottom0 = fence(b_top_in, b_bottom_in, top0, bottom0)
    top_in0, bottom_in0 = swap(top0, 0), swap(bottom0, 1)
    own_pairs = [
        (a_top, a_top_in),
        (a_bottom, a_bottom_in),
        (b_top, b_top_in),
        (b_bottom, b_bottom_in),
    ]
    own_layout = (((0, 0, half), (1, 0, half)), ((2, 0, half), (3, 0, half)))
    own_part0, own_part1, *gathered = act(own_pairs, held, None, 0, own_layout, total_rows)
    before1, after1, own_part0 = fence(before1, after1, own_part0)
    cut_top1, cut_bottom1 = before1[:half], after1[half:]
    far_top1, far_bottom1 = shift(cut_top1, 1), shift(cut_bottom1, -1)
    top_in0, bottom_in0, cut_top1, cut_bottom1 = fence(
        top_in0, bottom_in0, cut_top1, cut_bottom1
    )
    top0, bottom0 = add_halves(top0, top_in0, bottom0, bottom_in0)
    top_in0, bottom_in0 = swap(top0, 1), swap(bottom0, 0)
    far_top1, far_bottom1, top0, bottom0 = fence(far_top1, far_bottom1, top0, bottom0)
    top1, bottom1, all_rows = partial(
        (before1, far_top1, after1, far_bottom1),
        held,
        all_rows,
        base1,
        total_rows,
        True,
        PARTIAL_FLOPS,
    )
    top_in1, bottom_in1 = swap(top1, 0), swap(bottom1, 1)
    top_in0, bottom_in0, all_rows = fence(top_in0, bottom_in0, all_rows)
    layout = (
        ((0, 0, own_rows),),
        ((1, 0, own_rows),),
        ((0, own_rows, own_rows + half), (1, own_rows, own_rows + half)),
    )
    near_top0, near_bottom0, far0, *gathered = act(
        [(top0, top_in0), (bottom0, bottom_in0)], held, gathered, base0, layout, total_rows
    )
    home0 = [shift(near_top0, -1), shift(near_bottom0, 1), shift(far0, 2)]
    top_in1, bottom_in1, far0 = fence(top_in1, bottom_in1, far0)
    top1, bottom1 = add_halves(top1, top_in1, bottom1, bottom_in1)
    top_in1, bottom_in1 = swap(top1, 1), swap(bottom1, 0)
    *home0, top1, bottom1 = fence(*home0, top1, bottom1)
    total0 = total_of(own_part0, *home0, flops=TOTAL_FLOPS)
    top_in1, bottom_in1, top1, total0 = fence(top_in1, bottom_in1, top1, total0)
    near_top1, near_bottom1, far1, *gathered = act(
        [(top1, top_in1), (bottom1, bottom_in1)], held, gathered, base1, layout, total_rows
    )
    total0, far1 = fence(total0, far1)
    home1 = [shift(near_top1, -1), shift(near_bottom1, 1), shift(far1, 2)]
    back0 = to_experts(total0)
    all_hidden, all_both = gathered
    total0, all_rows, all_hidden, all_both = fence(total0, all_rows, all_hidden, all_both)
    gate_grad = dot(all_rows[:, :width], all_both[:, :units], CONTRACT_FIRST).astype(BF16)
    up_grad = dot(all_rows[:, :width], all_both[:, units:], CONTRACT_FIRST).astype(BF16)
    *home1, gate_grad, up_grad = fence(*home1, gate_grad, up_grad)
    total1 = total_of(own_part1, *home1)
    total1, back0 = fence(total1, back0)
    back1 = to_experts(total1)
    total1, all_hidden = fence(total1, all_hidden)
    down_grad = dot(all_hidden, all_rows[:, width:], CONTRACT_FIRST).astype(BF16)
    back1, down_grad = fence(back1, down_grad)
    input_grad, score_grad = final(usable, score, picks, [back0, back1])
    return input_grad, score_grad[None], gate_grad[None], up_grad[None], down_grad[None]


def solution(mesh):
    in_specs = (
        P(("gx", "gz"), "gy"),
        P(("gx", "gz"), "gy"),
        P(("gx", "gz"), None, None),
        P(("gx", "gz"), None),
        P(("gx", "gz"), None, None),
        P("gx", "gy", "gz"),
        P("gx", "gy", "gz"),
        P("gx", "gz", "gy"),
    )
    out_specs = (
        P(("gx", "gz"), "gy"),
        P(("gx", "gz"), None, None),
        P("gx", "gy", "gz"),
        P("gx", "gy", "gz"),
        P("gx", "gz", "gy"),
    )
    return jax.shard_map(local, mesh=mesh, in_specs=in_specs, out_specs=out_specs, check_vma=False)
```

```python
import functools
import jax
import jax.numpy as jnp
from jax import lax
from jax.experimental import pallas as pl
from jax.experimental.pallas import tpu as pltpu
from jax.sharding import PartitionSpec as P

CONTRACT_MIDDLE = (((1,), (0,)), ((), ()))
CONTRACT_LAST = (((1,), (1,)), ((), ()))
CONTRACT_FIRST = (((0,), (0,)), ((), ()))
CHUNKS = 2
LANES = 128
OWN_FLOPS = 20_000_000_000
PARTIAL_FLOPS = 20000000000
TOTAL_FLOPS = 20_000_000_000
VMEM_LIMIT = 20 * 1024 * 1024
BF16 = jnp.bfloat16
F32 = jnp.float32


def dot(left, right, dims=CONTRACT_MIDDLE):
    return lax.dot_general(left, right, dims, preferred_element_type=F32)


def shift(array, steps):
    size = lax.axis_size("gz")
    return lax.ppermute(array, "gz", [(i, (i + steps) % size) for i in range(size)])


def swap(array, bit):
    if bit:
        pairs = [(1, 2), (2, 1), (3, 0), (0, 3)]
    else:
        pairs = [(0, 1), (1, 0), (2, 3), (3, 2)]
    return lax.ppermute(array, "gy", pairs)


def add(left, right):
    return left.astype(F32) + right.astype(F32)


def fence(*arrays):
    return lax.optimization_barrier(arrays)


def to_experts(rows):
    return lax.all_to_all(rows, "gx", split_axis=0, concat_axis=0, tiled=True)


def call(kernel, outs, scratch, args, aliases=None, free=(), in_hbm=(), out_hbm=(), flops=1):
    vmem, hbm = pl.BlockSpec(memory_space=pltpu.VMEM), pl.BlockSpec(memory_space=pltpu.HBM)
    return pl.pallas_call(
        kernel,
        out_shape=[
            pltpu.HBM(*o) if i in out_hbm else jax.ShapeDtypeStruct(*o)
            for i, o in enumerate(outs)
        ],
        in_specs=[
            hbm if i in in_hbm else pl.BlockSpec(memory_space=pl.ANY) if i in free else vmem
            for i in range(len(args))
        ],
        out_specs=[hbm if i in out_hbm else vmem for i in range(len(outs))],
        scratch_shapes=scratch,
        input_output_aliases=aliases or {},
        cost_estimate=pl.CostEstimate(flops=flops, bytes_accessed=1, transcendentals=0),
        compiler_params=pltpu.CompilerParams(vmem_limit_bytes=VMEM_LIMIT),
    )(*args)


def hold_kernel(*refs):
    count = len(refs) // 2
    copies = [
        pltpu.make_async_copy(refs[i], refs[count + i], refs[-1].at[i]) for i in range(count)
    ]
    for copy in copies:
        copy.start()
    for copy in copies:
        copy.wait()


def hold(arrays):
    copies = pl.pallas_call(
        hold_kernel,
        out_shape=[pltpu.VMEM(a.shape, a.dtype) for a in arrays],
        in_specs=[pl.BlockSpec(memory_space=pltpu.HBM)] * len(arrays),
        out_specs=[pl.BlockSpec(memory_space=pltpu.VMEM)] * len(arrays),
        scratch_shapes=[pltpu.SemaphoreType.DMA((len(arrays),))],
        compiler_params=pltpu.CompilerParams(vmem_limit_bytes=VMEM_LIMIT),
    )(*arrays)
    return [pltpu.with_memory_space_constraint(a, pltpu.VMEM) for a in copies]


def cut_kernel(before, after, top, bottom, sems):
    half = top.shape[0]
    copies = [
        pltpu.make_async_copy(before.at[pl.ds(0, half)], top, sems.at[0]),
        pltpu.make_async_copy(after.at[pl.ds(half, half)], bottom, sems.at[1]),
    ]
    for copy in copies:
        copy.start()
    for copy in copies:
        copy.wait()


def cut(before, after):
    shape = (before.shape[0] // 2, before.shape[1])
    sems = pltpu.SemaphoreType.DMA((2,))
    return call(cut_kernel, [(shape, BF16)] * 2, [sems], [before, after], free=(0, 1))


def partial_kernel(pieces, base, aliased, held, *refs):
    inputs, refs = refs[:pieces], refs[pieces:]
    weights = refs[:3]
    refs = refs[4:] if aliased else refs[3:]
    if held:
        *outs, all_rows, rows, sems = refs
    else:
        *outs, all_rows, rows, sems, w_gate, w_up, w_down, w_sems = refs
        copies = [
            pltpu.make_async_copy(w, v, w_sems.at[i])
            for i, (w, v) in enumerate(zip(weights, (w_gate, w_up, w_down)))
        ]
        weights = (w_gate, w_up, w_down)
    w_copies = [] if held else copies
    width, units = weights[0].shape
    at, copies = 0, []
    for i, piece in enumerate(inputs):
        place = pl.ds(at, piece.shape[0])
        copies.append(pltpu.make_async_copy(piece, rows.at[place], sems.at[i]))
        at += piece.shape[0]
    for copy in copies + w_copies:
        copy.start()
    for copy in copies:
        copy.wait()
    keep = pltpu.make_async_copy(rows, all_rows.at[pl.ds(base, at)], sems.at[pieces])
    keep.start()
    size = at // len(outs)

    def store(k, left, dims):
        if not held:
            w_copies[k].wait()
        part = dot(left, weights[k][...], dims)
        for i, out in enumerate(outs):
            out[:, k * units : (k + 1) * units] = part[i * size : (i + 1) * size].astype(BF16)

    store(0, rows[:, :width], CONTRACT_MIDDLE)
    store(1, rows[:, :width], CONTRACT_MIDDLE)
    store(2, rows[:, width:], CONTRACT_LAST)
    keep.wait()


def partial(pieces, weights, all_rows, base, total_rows, held, flops=1):
    count = sum(p.shape[0] for p in pieces)
    width, units = weights[0].shape
    n = len(pieces)
    args = list(pieces) + list(weights)
    aliases, in_hbm = {}, () if held else (n, n + 1, n + 2)
    if all_rows is not None:
        aliases, in_hbm = {len(args): 2}, in_hbm + (n + 3,)
        args.append(all_rows)
    scratch = [pltpu.VMEM((count, 2 * width), BF16), pltpu.SemaphoreType.DMA((n + 1,))]
    if not held:
        scratch += [pltpu.VMEM(w.shape, BF16) for w in weights]
        scratch.append(pltpu.SemaphoreType.DMA((3,)))
    return call(
        functools.partial(partial_kernel, n, base, all_rows is not None, held),
        [((count // 2, 3 * units), BF16)] * 2 + [((total_rows, 2 * width), BF16)],
        scratch,
        args,
        aliases,
        tuple(range(n)),
        in_hbm,
        (2,),
        flops,
    )


def add_kernel(top, top_in, bottom, bottom_in, top_out, bottom_out):
    top_out[...] = add(top[...], top_in[...]).astype(BF16)
    bottom_out[...] = add(bottom[...], bottom_in[...]).astype(BF16)


def add_halves(top, top_in, bottom, bottom_in, flops=1):
    return call(
        add_kernel,
        [(top.shape, BF16), (bottom.shape, BF16)],
        [],
        [top, top_in, bottom, bottom_in],
        flops=flops,
    )


def two_parts(score):
    high = score.astype(BF16).astype(F32)
    lane = lax.broadcasted_iota(jnp.int32, (score.shape[0], LANES), 1)
    return jnp.where(lane == 0, high, jnp.where(lane == 1, score - high, 0.0)).astype(BF16)


def act_kernel(pairs, base, layout, aliased, *refs):
    values, refs = refs[: 2 * pairs], refs[2 * pairs :]
    w_gate, w_up = refs[:2]
    refs = refs[4:] if aliased else refs[2:]
    *outs, all_hidden, all_both, hidden_rows, both_rows, sems = refs
    width, units = w_gate.shape
    size = values[0].shape[0]
    scores = []
    for i in range(pairs):
        own, arrived = values[2 * i], values[2 * i + 1]
        place = slice(i * size, (i + 1) * size)
        gate_value = add(own[:, :units], arrived[:, :units])
        up_value = add(own[:, units : 2 * units], arrived[:, units : 2 * units])
        hidden_grad = add(own[:, 2 * units :], arrived[:, 2 * units :])
        sigmoid_gate = jax.nn.sigmoid(gate_value)
        activated = gate_value * sigmoid_gate
        hidden = (activated * up_value).astype(BF16)
        score_part = jnp.sum(hidden.astype(F32) * hidden_grad, axis=1, keepdims=True)
        scores.append(two_parts(score_part))
        hidden_rows[place] = hidden
        both_rows[place, :units] = (
            hidden_grad * up_value * sigmoid_gate * (1.0 + gate_value * (1.0 - sigmoid_gate))
        ).astype(BF16)
        both_rows[place, units:] = (hidden_grad * activated).astype(BF16)
    place = pl.ds(base, pairs * size)
    copies = [
        pltpu.make_async_copy(hidden_rows, all_hidden.at[place], sems.at[0]),
        pltpu.make_async_copy(both_rows, all_both.at[place], sems.at[1]),
    ]
    for copy in copies:
        copy.start()
    part = dot(both_rows[:, :units], w_gate[...], CONTRACT_LAST)
    part = (part + dot(both_rows[:, units:], w_up[...], CONTRACT_LAST)).astype(BF16)
    for out, blocks in zip(outs, layout):
        at = 0
        for i, first, last in blocks:
            end = at + last - first
            out[at:end, :width] = part[i * size + first : i * size + last]
            out[at:end, width:] = scores[i][first:last]
            at = end
    for copy in copies:
        copy.wait()


def act(pairs, weights, gathered, base, layout, total_rows):
    width, units = weights[0].shape
    rows = sum(own.shape[0] for own, _ in pairs)
    args = [a for pair in pairs for a in pair] + [weights[0], weights[1]]
    outs = [
        ((sum(last - first for _, first, last in blocks), width + LANES), BF16)
        for blocks in layout
    ]
    n = len(outs)
    outs += [((total_rows, units), BF16), ((total_rows, 2 * units), BF16)]
    aliases, in_hbm = {}, ()
    if gathered is not None:
        in_hbm = (len(args), len(args) + 1)
        aliases = {in_hbm[0]: n, in_hbm[1]: n + 1}
        args += list(gathered)
    return call(
        functools.partial(act_kernel, len(pairs), base, layout, gathered is not None),
        outs,
        [
            pltpu.VMEM((rows, units), BF16),
            pltpu.VMEM((rows, 2 * units), BF16),
            pltpu.SemaphoreType.DMA((2,)),
        ],
        args,
        aliases,
        (),
        in_hbm,
        (n, n + 1),
    )


def total_kernel(width, own, first, second, third, out):
    total = add(own[...], first[...]) + add(second[...], third[...])
    out[:, :width] = total[:, :width].astype(BF16)
    out[:, width:] = two_parts(jnp.sum(total[:, width:], axis=1, keepdims=True))


def total_of(own, first, second, third, flops=1):
    kernel = functools.partial(total_kernel, own.shape[1] - LANES)
    args = [own, first, second, third]
    return call(kernel, [(own.shape, BF16)], [], args, flops=flops)[0]


def final_kernel(chunks, usable, score, *refs):
    picks, backs = refs[:chunks], refs[chunks : 2 * chunks]
    input_grad, score_grad = refs[2 * chunks :]
    width = input_grad.shape[1]
    experts, slots = score.shape
    rows = backs[0].shape[0]
    part_slots = rows // experts
    total = sum(dot(p[...], b[:, :width], CONTRACT_FIRST) for p, b in zip(picks, backs))
    input_grad[...] = total.astype(BF16)
    row = lax.broadcasted_iota(jnp.int32, (rows, slots), 0)
    column = lax.broadcasted_iota(jnp.int32, (rows, slots), 1)
    expert = (
        lax.broadcasted_iota(jnp.int32, (experts, rows), 1) // part_slots
        == lax.broadcasted_iota(jnp.int32, (experts, rows), 0)
    ).astype(F32).astype(BF16)
    table = jnp.zeros((experts, slots), F32)
    for c, back in enumerate(backs):
        for k in range(2):
            value = back[:, width + k : width + k + 1].astype(F32)
            spread = jnp.where(column == c * part_slots + row % part_slots, value, 0.0)
            table += dot(expert, spread.astype(BF16))
    score_grad[...] = jnp.where(usable[...] > 0, table / score[...], 0.0)


def final(usable, score, picks, backs):
    group, width = picks[0].shape[1], backs[0].shape[1] - LANES
    return call(
        functools.partial(final_kernel, len(picks)),
        [((group, width), BF16), (score.shape, F32)],
        [],
        [usable.astype(jnp.int32), score.astype(F32), *picks, *backs],
    )


def local(
    tokens, grad_out, slot_token, slot_count, slot_score, gate_weight, up_weight, down_weight
):
    chosen = slot_token[0]
    counts = slot_count[0]
    experts, slots = chosen.shape
    group, width = tokens.shape
    usable = jnp.arange(slots, dtype=jnp.int32)[None, :] < counts[:, None]
    score = slot_score[0]
    picked = (
        chosen[:, :, None] == jnp.arange(group, dtype=jnp.int32)[None, None, :]
    ) & usable[:, :, None]
    zero = jnp.zeros((), BF16)
    pick = jnp.where(picked, jnp.ones((), BF16), zero)
    pick_scaled = jnp.where(picked, score[:, :, None], zero)

    weights = [
        pltpu.with_memory_space_constraint(w[0], pltpu.HBM)
        for w in (gate_weight, up_weight, down_weight)
    ]
    units = weights[2].shape[0]
    part_slots = slots // CHUNKS
    own_rows = experts * part_slots
    half = own_rows // 2
    total_rows = own_rows * CHUNKS * lax.axis_size("gz")

    def chunk_of(array, c):
        return array[:, c * part_slots : (c + 1) * part_slots].reshape(own_rows, -1)

    picks = [chunk_of(pick, c) for c in range(CHUNKS)]
    scaled_picks = [chunk_of(pick_scaled, c) for c in range(CHUNKS)]

    def dispatch(pick_x, pick_g):
        return jnp.concatenate(
            [dot(pick_x, tokens).astype(BF16), dot(pick_g, grad_out).astype(BF16)], axis=1
        )

    sent0 = dispatch(picks[0], scaled_picks[0])
    own0 = to_experts(sent0)
    sent0, pick1 = fence(sent0, picks[1])
    sent1 = dispatch(pick1, scaled_picks[1])
    own0, sent1 = fence(own0, sent1)
    before0, after0 = shift(own0, 1), shift(own0, -1)
    own1 = to_experts(sent1)
    a_top, a_bottom, all_rows = partial((own0,), weights, None, 0, total_rows, False)
    a_top_in, a_bottom_in = swap(a_top, 0), swap(a_bottom, 1)
    a_top, a_bottom = add_halves(a_top, a_top_in, a_bottom, a_bottom_in)
    a_top_in, a_bottom_in = swap(a_top, 1), swap(a_bottom, 0)
    before0, after0, all_rows, a_top, own1 = fence(before0, after0, all_rows, a_top, own1)
    cut_top0, cut_bottom0 = cut(before0, after0)
    far_top0, far_bottom0 = shift(cut_top0, 1), shift(cut_bottom0, -1)
    own1, all_rows, cut_top0 = fence(own1, all_rows, cut_top0)
    b_top, b_bottom, all_rows = partial(
        (own1,), weights, all_rows, own_rows, total_rows, False, OWN_FLOPS
    )
    a_top_in, a_bottom_in, b_top, b_bottom = fence(a_top_in, a_bottom_in, b_top, b_bottom)
    b_top_in, b_bottom_in = swap(b_top, 0), swap(b_bottom, 1)
    b_top, *weights = fence(b_top, *weights)
    held = hold(weights)
    far_top0, far_bottom0, own1, *held = fence(far_top0, far_bottom0, own1, *held)
    before1, after1 = shift(own1, 1), shift(own1, -1)
    b_top_in, b_bottom_in, far_top0 = fence(b_top_in, b_bottom_in, far_top0)
    b_top, b_bottom = add_halves(b_top, b_top_in, b_bottom, b_bottom_in, OWN_FLOPS)
    b_top_in, b_bottom_in = swap(b_top, 1), swap(b_bottom, 0)
    far_top0, far_bottom0, b_top = fence(far_top0, far_bottom0, b_top)
    base0, base1 = CHUNKS * own_rows, (CHUNKS + 3) * own_rows
    top0, bottom0, all_rows = partial(
        (before0, far_top0, after0, far_bottom0), held, all_rows, base0, total_rows, True
    )
    b_top_in, b_bottom_in, top0, bottom0 = fence(b_top_in, b_bottom_in, top0, bottom0)
    top_in0, bottom_in0 = swap(top0, 0), swap(bottom0, 1)
    own_pairs = [
        (a_top, a_top_in),
        (a_bottom, a_bottom_in),
        (b_top, b_top_in),
        (b_bottom, b_bottom_in),
    ]
    own_layout = (((0, 0, half), (1, 0, half)), ((2, 0, half), (3, 0, half)))
    own_part0, own_part1, *gathered = act(own_pairs, held, None, 0, own_layout, total_rows)
    before1, after1, own_part0 = fence(before1, after1, own_part0)
    cut_top1, cut_bottom1 = cut(before1, after1)
    far_top1, far_bottom1 = shift(cut_top1, 1), shift(cut_bottom1, -1)
    top_in0, bottom_in0, cut_top1, cut_bottom1 = fence(
        top_in0, bottom_in0, cut_top1, cut_bottom1
    )
    top0, bottom0 = add_halves(top0, top_in0, bottom0, bottom_in0)
    top_in0, bottom_in0 = swap(top0, 1), swap(bottom0, 0)
    far_top1, far_bottom1, top0, bottom0 = fence(far_top1, far_bottom1, top0, bottom0)
    top1, bottom1, all_rows = partial(
        (before1, far_top1, after1, far_bottom1),
        held,
        all_rows,
        base1,
        total_rows,
        True,
        PARTIAL_FLOPS,
    )
    top_in1, bottom_in1 = swap(top1, 0), swap(bottom1, 1)
    top_in0, bottom_in0, all_rows = fence(top_in0, bottom_in0, all_rows)
    layout = (
        ((0, 0, own_rows),),
        ((1, 0, own_rows),),
        ((0, own_rows, own_rows + half), (1, own_rows, own_rows + half)),
    )
    near_top0, near_bottom0, far0, *gathered = act(
        [(top0, top_in0), (bottom0, bottom_in0)], held, gathered, base0, layout, total_rows
    )
    home0 = [shift(near_top0, -1), shift(near_bottom0, 1), shift(far0, 2)]
    top_in1, bottom_in1, far0 = fence(top_in1, bottom_in1, far0)
    top1, bottom1 = add_halves(top1, top_in1, bottom1, bottom_in1)
    top_in1, bottom_in1 = swap(top1, 1), swap(bottom1, 0)
    *home0, top1, bottom1 = fence(*home0, top1, bottom1)
    total0 = total_of(own_part0, *home0, flops=TOTAL_FLOPS)
    top_in1, bottom_in1, top1, total0 = fence(top_in1, bottom_in1, top1, total0)
    near_top1, near_bottom1, far1, *gathered = act(
        [(top1, top_in1), (bottom1, bottom_in1)], held, gathered, base1, layout, total_rows
    )
    total0, far1 = fence(total0, far1)
    home1 = [shift(near_top1, -1), shift(near_bottom1, 1), shift(far1, 2)]
    back0 = to_experts(total0)
    all_hidden, all_both = gathered
    total0, all_rows, all_hidden, all_both = fence(total0, all_rows, all_hidden, all_both)
    gate_grad = dot(all_rows[:, :width], all_both[:, :units], CONTRACT_FIRST).astype(BF16)
    up_grad = dot(all_rows[:, :width], all_both[:, units:], CONTRACT_FIRST).astype(BF16)
    *home1, gate_grad, up_grad = fence(*home1, gate_grad, up_grad)
    total1 = total_of(own_part1, *home1)
    total1, back0 = fence(total1, back0)
    back1 = to_experts(total1)
    total1, all_hidden = fence(total1, all_hidden)
    down_grad = dot(all_hidden, all_rows[:, width:], CONTRACT_FIRST).astype(BF16)
    back1, down_grad = fence(back1, down_grad)
    input_grad, score_grad = final(usable, score, picks, [back0, back1])
    return input_grad, score_grad[None], gate_grad[None], up_grad[None], down_grad[None]


def solution(mesh):
    in_specs = (
        P(("gx", "gz"), "gy"),
        P(("gx", "gz"), "gy"),
        P(("gx", "gz"), None, None),
        P(("gx", "gz"), None),
        P(("gx", "gz"), None, None),
        P("gx", "gy", "gz"),
        P("gx", "gy", "gz"),
        P("gx", "gz", "gy"),
    )
    out_specs = (
        P(("gx", "gz"), "gy"),
        P(("gx", "gz"), None, None),
        P("gx", "gy", "gz"),
        P("gx", "gy", "gz"),
        P("gx", "gz", "gy"),
    )
    return jax.shard_map(local, mesh=mesh, in_specs=in_specs, out_specs=out_specs, check_vma=False)
```

```python
import functools
import jax
import jax.numpy as jnp
from jax import lax
from jax.experimental import pallas as pl
from jax.experimental.pallas import tpu as pltpu
from jax.sharding import PartitionSpec as P

CONTRACT_MIDDLE = (((1,), (0,)), ((), ()))
CONTRACT_LAST = (((1,), (1,)), ((), ()))
CONTRACT_FIRST = (((0,), (0,)), ((), ()))
CHUNKS = 2
LANES = 128
OWN_FLOPS = 20_000_000_000
PARTIAL_FLOPS = 20000000000
TOTAL_FLOPS = 20_000_000_000
VMEM_LIMIT = 20 * 1024 * 1024
BF16 = jnp.bfloat16
F32 = jnp.float32


def dot(left, right, dims=CONTRACT_MIDDLE):
    return lax.dot_general(left, right, dims, preferred_element_type=F32)


def shift(array, steps):
    size = lax.axis_size("gz")
    return lax.ppermute(array, "gz", [(i, (i + steps) % size) for i in range(size)])


def swap(array, bit):
    if bit:
        pairs = [(1, 2), (2, 1), (3, 0), (0, 3)]
    else:
        pairs = [(0, 1), (1, 0), (2, 3), (3, 2)]
    return lax.ppermute(array, "gy", pairs)


def add(left, right):
    return left.astype(F32) + right.astype(F32)


def fence(*arrays):
    return lax.optimization_barrier(arrays)


def to_experts(rows):
    return lax.all_to_all(rows, "gx", split_axis=0, concat_axis=0, tiled=True)


def call(kernel, outs, scratch, args, aliases=None, free=(), in_hbm=(), out_hbm=(), flops=1):
    vmem, hbm = pl.BlockSpec(memory_space=pltpu.VMEM), pl.BlockSpec(memory_space=pltpu.HBM)
    return pl.pallas_call(
        kernel,
        out_shape=[
            pltpu.HBM(*o) if i in out_hbm else jax.ShapeDtypeStruct(*o)
            for i, o in enumerate(outs)
        ],
        in_specs=[
            hbm if i in in_hbm else pl.BlockSpec(memory_space=pl.ANY) if i in free else vmem
            for i in range(len(args))
        ],
        out_specs=[hbm if i in out_hbm else vmem for i in range(len(outs))],
        scratch_shapes=scratch,
        input_output_aliases=aliases or {},
        cost_estimate=pl.CostEstimate(flops=flops, bytes_accessed=1, transcendentals=0),
        compiler_params=pltpu.CompilerParams(vmem_limit_bytes=VMEM_LIMIT),
    )(*args)


def hold_kernel(*refs):
    count = len(refs) // 2
    copies = [
        pltpu.make_async_copy(refs[i], refs[count + i], refs[-1].at[i]) for i in range(count)
    ]
    for copy in copies:
        copy.start()
    for copy in copies:
        copy.wait()


def hold(arrays):
    copies = pl.pallas_call(
        hold_kernel,
        out_shape=[pltpu.VMEM(a.shape, a.dtype) for a in arrays],
        in_specs=[pl.BlockSpec(memory_space=pltpu.HBM)] * len(arrays),
        out_specs=[pl.BlockSpec(memory_space=pltpu.VMEM)] * len(arrays),
        scratch_shapes=[pltpu.SemaphoreType.DMA((len(arrays),))],
        compiler_params=pltpu.CompilerParams(vmem_limit_bytes=VMEM_LIMIT),
    )(*arrays)
    return [pltpu.with_memory_space_constraint(a, pltpu.VMEM) for a in copies]


def cut_kernel(before, after, top, bottom, sems):
    half = top.shape[0]
    copies = [
        pltpu.make_async_copy(before.at[pl.ds(0, half)], top, sems.at[0]),
        pltpu.make_async_copy(after.at[pl.ds(half, half)], bottom, sems.at[1]),
    ]
    for copy in copies:
        copy.start()
    for copy in copies:
        copy.wait()


def cut(before, after):
    shape = (before.shape[0] // 2, before.shape[1])
    sems = pltpu.SemaphoreType.DMA((2,))
    return call(cut_kernel, [(shape, BF16)] * 2, [sems], [before, after], free=(0, 1))


def partial_kernel(pieces, base, aliased, held, *refs):
    inputs, refs = refs[:pieces], refs[pieces:]
    weights = refs[:3]
    refs = refs[4:] if aliased else refs[3:]
    if held:
        *outs, all_rows, rows, sems = refs
    else:
        *outs, all_rows, rows, sems, w_gate, w_up, w_down, w_sems = refs
        copies = [
            pltpu.make_async_copy(w, v, w_sems.at[i])
            for i, (w, v) in enumerate(zip(weights, (w_gate, w_up, w_down)))
        ]
        weights = (w_gate, w_up, w_down)
    w_copies = [] if held else copies
    width, units = weights[0].shape
    at, copies = 0, []
    for i, piece in enumerate(inputs):
        place = pl.ds(at, piece.shape[0])
        copies.append(pltpu.make_async_copy(piece, rows.at[place], sems.at[i]))
        at += piece.shape[0]
    for copy in copies + w_copies:
        copy.start()
    for copy in copies:
        copy.wait()
    keep = pltpu.make_async_copy(rows, all_rows.at[pl.ds(base, at)], sems.at[pieces])
    keep.start()
    size = at // len(outs)

    def store(k, left, dims):
        if not held:
            w_copies[k].wait()
        part = dot(left, weights[k][...], dims)
        for i, out in enumerate(outs):
            out[:, k * units : (k + 1) * units] = part[i * size : (i + 1) * size].astype(BF16)

    store(0, rows[:, :width], CONTRACT_MIDDLE)
    store(1, rows[:, :width], CONTRACT_MIDDLE)
    store(2, rows[:, width:], CONTRACT_LAST)
    keep.wait()


def partial(pieces, weights, all_rows, base, total_rows, held, flops=1):
    count = sum(p.shape[0] for p in pieces)
    width, units = weights[0].shape
    n = len(pieces)
    args = list(pieces) + list(weights)
    aliases, in_hbm = {}, () if held else (n, n + 1, n + 2)
    if all_rows is not None:
        aliases, in_hbm = {len(args): 2}, in_hbm + (n + 3,)
        args.append(all_rows)
    scratch = [pltpu.VMEM((count, 2 * width), BF16), pltpu.SemaphoreType.DMA((n + 1,))]
    if not held:
        scratch += [pltpu.VMEM(w.shape, BF16) for w in weights]
        scratch.append(pltpu.SemaphoreType.DMA((3,)))
    return call(
        functools.partial(partial_kernel, n, base, all_rows is not None, held),
        [((count // 2, 3 * units), BF16)] * 2 + [((total_rows, 2 * width), BF16)],
        scratch,
        args,
        aliases,
        tuple(range(n)),
        in_hbm,
        (2,),
        flops,
    )


def add_kernel(top, top_in, bottom, bottom_in, top_out, bottom_out):
    top_out[...] = add(top[...], top_in[...]).astype(BF16)
    bottom_out[...] = add(bottom[...], bottom_in[...]).astype(BF16)


def add_halves(top, top_in, bottom, bottom_in, flops=1):
    return call(
        add_kernel,
        [(top.shape, BF16), (bottom.shape, BF16)],
        [],
        [top, top_in, bottom, bottom_in],
        flops=flops,
    )


def two_parts(score):
    high = score.astype(BF16).astype(F32)
    lane = lax.broadcasted_iota(jnp.int32, (score.shape[0], LANES), 1)
    return jnp.where(lane == 0, high, jnp.where(lane == 1, score - high, 0.0)).astype(BF16)


def act_kernel(pairs, base, layout, aliased, *refs):
    values, refs = refs[: 2 * pairs], refs[2 * pairs :]
    w_gate, w_up = refs[:2]
    refs = refs[4:] if aliased else refs[2:]
    *outs, all_hidden, all_both, hidden_rows, both_rows, sems = refs
    width, units = w_gate.shape
    size = values[0].shape[0]
    scores = []
    for i in range(pairs):
        own, arrived = values[2 * i], values[2 * i + 1]
        place = slice(i * size, (i + 1) * size)
        gate_value = add(own[:, :units], arrived[:, :units])
        up_value = add(own[:, units : 2 * units], arrived[:, units : 2 * units])
        hidden_grad = add(own[:, 2 * units :], arrived[:, 2 * units :])
        sigmoid_gate = jax.nn.sigmoid(gate_value)
        activated = gate_value * sigmoid_gate
        hidden = (activated * up_value).astype(BF16)
        score_part = jnp.sum(hidden.astype(F32) * hidden_grad, axis=1, keepdims=True)
        scores.append(two_parts(score_part))
        hidden_rows[place] = hidden
        both_rows[place, :units] = (
            hidden_grad * up_value * sigmoid_gate * (1.0 + gate_value * (1.0 - sigmoid_gate))
        ).astype(BF16)
        both_rows[place, units:] = (hidden_grad * activated).astype(BF16)
    place = pl.ds(base, pairs * size)
    copies = [
        pltpu.make_async_copy(hidden_rows, all_hidden.at[place], sems.at[0]),
        pltpu.make_async_copy(both_rows, all_both.at[place], sems.at[1]),
    ]
    for copy in copies:
        copy.start()
    part = dot(both_rows[:, :units], w_gate[...], CONTRACT_LAST)
    part = (part + dot(both_rows[:, units:], w_up[...], CONTRACT_LAST)).astype(BF16)
    for out, blocks in zip(outs, layout):
        at = 0
        for i, first, last in blocks:
            end = at + last - first
            out[at:end, :width] = part[i * size + first : i * size + last]
            out[at:end, width:] = scores[i][first:last]
            at = end
    for copy in copies:
        copy.wait()


def act(pairs, weights, gathered, base, layout, total_rows):
    width, units = weights[0].shape
    rows = sum(own.shape[0] for own, _ in pairs)
    args = [a for pair in pairs for a in pair] + [weights[0], weights[1]]
    outs = [
        ((sum(last - first for _, first, last in blocks), width + LANES), BF16)
        for blocks in layout
    ]
    n = len(outs)
    outs += [((total_rows, units), BF16), ((total_rows, 2 * units), BF16)]
    aliases, in_hbm = {}, ()
    if gathered is not None:
        in_hbm = (len(args), len(args) + 1)
        aliases = {in_hbm[0]: n, in_hbm[1]: n + 1}
        args += list(gathered)
    return call(
        functools.partial(act_kernel, len(pairs), base, layout, gathered is not None),
        outs,
        [
            pltpu.VMEM((rows, units), BF16),
            pltpu.VMEM((rows, 2 * units), BF16),
            pltpu.SemaphoreType.DMA((2,)),
        ],
        args,
        aliases,
        (),
        in_hbm,
        (n, n + 1),
    )


def total_kernel(width, own, first, second, third, out):
    total = add(own[...], first[...]) + add(second[...], third[...])
    out[:, :width] = total[:, :width].astype(BF16)
    out[:, width:] = two_parts(jnp.sum(total[:, width:], axis=1, keepdims=True))


def total_of(own, first, second, third, flops=1):
    kernel = functools.partial(total_kernel, own.shape[1] - LANES)
    args = [own, first, second, third]
    return call(kernel, [(own.shape, BF16)], [], args, flops=flops)[0]


def final_kernel(chunks, usable, score, *refs):
    picks, backs = refs[:chunks], refs[chunks : 2 * chunks]
    input_grad, score_grad, block, sems = refs[2 * chunks :]
    width = input_grad.shape[1]
    copies = []
    for i in range(2):
        place = slice(i * width // 2, (i + 1) * width // 2)
        total = sum(dot(p[...], b[:, place], CONTRACT_FIRST) for p, b in zip(picks, backs))
        block[i] = total.astype(BF16)
        target = input_grad.at[:, pl.ds(i * width // 2, width // 2)]
        copies.append(pltpu.make_async_copy(block.at[i], target, sems.at[i]))
        copies[i].start()
    experts, slots = score.shape
    rows = backs[0].shape[0]
    part_slots = rows // experts
    row = lax.broadcasted_iota(jnp.int32, (rows, slots), 0)
    column = lax.broadcasted_iota(jnp.int32, (rows, slots), 1)
    expert = (
        lax.broadcasted_iota(jnp.int32, (experts, rows), 1) // part_slots
        == lax.broadcasted_iota(jnp.int32, (experts, rows), 0)
    ).astype(F32).astype(BF16)
    table = jnp.zeros((experts, slots), F32)
    for c, back in enumerate(backs):
        for k in range(2):
            value = back[:, width + k : width + k + 1].astype(F32)
            spread = jnp.where(column == c * part_slots + row % part_slots, value, 0.0)
            table += dot(expert, spread.astype(BF16))
    score_grad[...] = jnp.where(usable[...] > 0, table / score[...], 0.0)
    for copy in copies:
        copy.wait()


def final(usable, score, picks, backs):
    group, width = picks[0].shape[1], backs[0].shape[1] - LANES
    return call(
        functools.partial(final_kernel, len(picks)),
        [((group, width), BF16), (score.shape, F32)],
        [pltpu.VMEM((2, group, width // 2), BF16), pltpu.SemaphoreType.DMA((2,))],
        [usable.astype(jnp.int32), score.astype(F32), *picks, *backs],
        out_hbm=(0,),
    )


def local(
    tokens, grad_out, slot_token, slot_count, slot_score, gate_weight, up_weight, down_weight
):
    chosen = slot_token[0]
    counts = slot_count[0]
    experts, slots = chosen.shape
    group, width = tokens.shape
    usable = jnp.arange(slots, dtype=jnp.int32)[None, :] < counts[:, None]
    score = slot_score[0]
    picked = (
        chosen[:, :, None] == jnp.arange(group, dtype=jnp.int32)[None, None, :]
    ) & usable[:, :, None]
    zero = jnp.zeros((), BF16)
    pick = jnp.where(picked, jnp.ones((), BF16), zero)
    pick_scaled = jnp.where(picked, score[:, :, None], zero)

    weights = [
        pltpu.with_memory_space_constraint(w[0], pltpu.HBM)
        for w in (gate_weight, up_weight, down_weight)
    ]
    units = weights[2].shape[0]
    part_slots = slots // CHUNKS
    own_rows = experts * part_slots
    half = own_rows // 2
    total_rows = own_rows * CHUNKS * lax.axis_size("gz")

    def chunk_of(array, c):
        return array[:, c * part_slots : (c + 1) * part_slots].reshape(own_rows, -1)

    picks = [chunk_of(pick, c) for c in range(CHUNKS)]
    scaled_picks = [chunk_of(pick_scaled, c) for c in range(CHUNKS)]

    def dispatch(pick_x, pick_g):
        return jnp.concatenate(
            [dot(pick_x, tokens).astype(BF16), dot(pick_g, grad_out).astype(BF16)], axis=1
        )

    sent0 = dispatch(picks[0], scaled_picks[0])
    own0 = to_experts(sent0)
    sent0, pick1 = fence(sent0, picks[1])
    sent1 = dispatch(pick1, scaled_picks[1])
    own0, sent1 = fence(own0, sent1)
    before0, after0 = shift(own0, 1), shift(own0, -1)
    own1 = to_experts(sent1)
    a_top, a_bottom, all_rows = partial((own0,), weights, None, 0, total_rows, False)
    a_top_in, a_bottom_in = swap(a_top, 0), swap(a_bottom, 1)
    a_top, a_bottom = add_halves(a_top, a_top_in, a_bottom, a_bottom_in)
    a_top_in, a_bottom_in = swap(a_top, 1), swap(a_bottom, 0)
    before0, after0, all_rows, a_top, own1 = fence(before0, after0, all_rows, a_top, own1)
    cut_top0, cut_bottom0 = cut(before0, after0)
    far_top0, far_bottom0 = shift(cut_top0, 1), shift(cut_bottom0, -1)
    own1, all_rows, cut_top0 = fence(own1, all_rows, cut_top0)
    b_top, b_bottom, all_rows = partial(
        (own1,), weights, all_rows, own_rows, total_rows, False, OWN_FLOPS
    )
    a_top_in, a_bottom_in, b_top, b_bottom = fence(a_top_in, a_bottom_in, b_top, b_bottom)
    b_top_in, b_bottom_in = swap(b_top, 0), swap(b_bottom, 1)
    b_top, *weights = fence(b_top, *weights)
    held = hold(weights)
    far_top0, far_bottom0, own1, *held = fence(far_top0, far_bottom0, own1, *held)
    before1, after1 = shift(own1, 1), shift(own1, -1)
    b_top_in, b_bottom_in, far_top0 = fence(b_top_in, b_bottom_in, far_top0)
    b_top, b_bottom = add_halves(b_top, b_top_in, b_bottom, b_bottom_in, OWN_FLOPS)
    b_top_in, b_bottom_in = swap(b_top, 1), swap(b_bottom, 0)
    far_top0, far_bottom0, b_top = fence(far_top0, far_bottom0, b_top)
    base0, base1 = CHUNKS * own_rows, (CHUNKS + 3) * own_rows
    top0, bottom0, all_rows = partial(
        (before0, far_top0, after0, far_bottom0), held, all_rows, base0, total_rows, True
    )
    b_top_in, b_bottom_in, top0, bottom0 = fence(b_top_in, b_bottom_in, top0, bottom0)
    top_in0, bottom_in0 = swap(top0, 0), swap(bottom0, 1)
    own_pairs = [
        (a_top, a_top_in),
        (a_bottom, a_bottom_in),
        (b_top, b_top_in),
        (b_bottom, b_bottom_in),
    ]
    own_layout = (((0, 0, half), (1, 0, half)), ((2, 0, half), (3, 0, half)))
    own_part0, own_part1, *gathered = act(own_pairs, held, None, 0, own_layout, total_rows)
    before1, after1, own_part0 = fence(before1, after1, own_part0)
    cut_top1, cut_bottom1 = cut(before1, after1)
    far_top1, far_bottom1 = shift(cut_top1, 1), shift(cut_bottom1, -1)
    top_in0, bottom_in0, cut_top1, cut_bottom1 = fence(
        top_in0, bottom_in0, cut_top1, cut_bottom1
    )
    top0, bottom0 = add_halves(top0, top_in0, bottom0, bottom_in0)
    top_in0, bottom_in0 = swap(top0, 1), swap(bottom0, 0)
    far_top1, far_bottom1, top0, bottom0 = fence(far_top1, far_bottom1, top0, bottom0)
    top1, bottom1, all_rows = partial(
        (before1, far_top1, after1, far_bottom1),
        held,
        all_rows,
        base1,
        total_rows,
        True,
        PARTIAL_FLOPS,
    )
    top_in1, bottom_in1 = swap(top1, 0), swap(bottom1, 1)
    top_in0, bottom_in0, all_rows = fence(top_in0, bottom_in0, all_rows)
    layout = (
        ((0, 0, own_rows),),
        ((1, 0, own_rows),),
        ((0, own_rows, own_rows + half), (1, own_rows, own_rows + half)),
    )
    near_top0, near_bottom0, far0, *gathered = act(
        [(top0, top_in0), (bottom0, bottom_in0)], held, gathered, base0, layout, total_rows
    )
    home0 = [shift(near_top0, -1), shift(near_bottom0, 1), shift(far0, 2)]
    top_in1, bottom_in1, far0 = fence(top_in1, bottom_in1, far0)
    top1, bottom1 = add_halves(top1, top_in1, bottom1, bottom_in1)
    top_in1, bottom_in1 = swap(top1, 1), swap(bottom1, 0)
    *home0, top1, bottom1 = fence(*home0, top1, bottom1)
    total0 = total_of(own_part0, *home0, flops=TOTAL_FLOPS)
    top_in1, bottom_in1, top1, total0 = fence(top_in1, bottom_in1, top1, total0)
    near_top1, near_bottom1, far1, *gathered = act(
        [(top1, top_in1), (bottom1, bottom_in1)], held, gathered, base1, layout, total_rows
    )
    total0, far1 = fence(total0, far1)
    home1 = [shift(near_top1, -1), shift(near_bottom1, 1), shift(far1, 2)]
    back0 = to_experts(total0)
    all_hidden, all_both = gathered
    total0, all_rows, all_hidden, all_both = fence(total0, all_rows, all_hidden, all_both)
    gate_grad = dot(all_rows[:, :width], all_both[:, :units], CONTRACT_FIRST).astype(BF16)
    up_grad = dot(all_rows[:, :width], all_both[:, units:], CONTRACT_FIRST).astype(BF16)
    *home1, gate_grad, up_grad = fence(*home1, gate_grad, up_grad)
    total1 = total_of(own_part1, *home1)
    total1, back0 = fence(total1, back0)
    back1 = to_experts(total1)
    total1, all_hidden = fence(total1, all_hidden)
    down_grad = dot(all_hidden, all_rows[:, width:], CONTRACT_FIRST).astype(BF16)
    back1, down_grad = fence(back1, down_grad)
    input_grad, score_grad = final(usable, score, picks, [back0, back1])
    return input_grad, score_grad[None], gate_grad[None], up_grad[None], down_grad[None]


def solution(mesh):
    in_specs = (
        P(("gx", "gz"), "gy"),
        P(("gx", "gz"), "gy"),
        P(("gx", "gz"), None, None),
        P(("gx", "gz"), None),
        P(("gx", "gz"), None, None),
        P("gx", "gy", "gz"),
        P("gx", "gy", "gz"),
        P("gx", "gz", "gy"),
    )
    out_specs = (
        P(("gx", "gz"), "gy"),
        P(("gx", "gz"), None, None),
        P("gx", "gy", "gz"),
        P("gx", "gy", "gz"),
        P("gx", "gz", "gy"),
    )
    return jax.shard_map(local, mesh=mesh, in_specs=in_specs, out_specs=out_specs, check_vma=False)
```
